512 devices in a mesh: gz: 32 (over z, core), xy: 16 (over x, y).
Axes of the slice: x: 4, y: 4, z: 16, core: 2. Of those that a mesh axis runs over, the one named last changes fastest.
Arguments:
- fields: float32 [4, 128, 128, 1024], P(None, 'gz', 'xy'), may hold values from -6 to 6
- conductance: float32 [4, 128, 128, 1024], P(None, 'gz', 'xy'), may hold values from 1000 to 10000
- lateral: float32 [4], replicated, may hold values from 0.05 to 0.24
- partition: float32 [3], replicated, may hold values from 0.1 to 0.8
- arm_step: float32 [3, 64, 64], replicated, may hold values from -0.2 to 0.95
- profiles: float32 [3, 8192, 64, 128], P(None, ('gz', 'xy')), may hold values from -6 to 6
- tile_ids: int32 [512, 16], P(('gz', 'xy')), may hold values from 0 to 255, as said below
- tile_count: int32 [512], P(('gz', 'xy')), may hold values from 0 to 16, as said below
Outputs:
- new_fields: float32 [4, 128, 128, 1024], P(None, 'gz', 'xy')
- new_profiles: float32 [3, 8192, 64, 128], P(None, ('gz', 'xy'))
The draws below stay inside these ranges and needn't reach their ends.
Inputs may be any that keep to these rules, and one draw needn't show every extreme that they name: `tile_ids`: the first tile_count entries of a device's row are distinct; an entry numbers a tile of that device's own block. `tile_count`: some device has exactly 16; the counts of two devices with the same gz index whose xy indices differ by 8 add up to at most 16.
All inputs are finite; a program needn't handle non-finite values.
Results may differ from the reference program's by a relative error of at most 0.0003.
Values sent between devices are 32-bit elements; how exact they have to be, the bound alone decides.
A program may use at most 64 MiB of HBM per device.

```python
import math
import jax
import jax.numpy as jnp
from jax import lax

CZ = 4
CX = 8
NY = 1024
MAXT = 16
ARM = 64
TILE = 128
SUB = 16
NZ = 128
NX = 128
RANKS = 512
SLOTS = 8192
NTILE = 256
HALF_XY = 8
N_GZ = 32
N_XY = 16


def draw_fields(key, part):
    shape = (4, NZ, NX * 0 + CX * (NX // CX), NY)
    return jnp.clip(jax.random.normal(jax.random.fold_in(key, 41), shape, jnp.float32), -6.0, 6.0)


def draw_arm_step(key, part):
    noise_part = jnp.clip(jax.random.normal(jax.random.fold_in(key, 11), (3, ARM, ARM), jnp.float32), -4.0, 4.0)
    diagonal_mask = (jnp.arange(ARM)[:, None] == jnp.arange(ARM)[None, :]).astype(jnp.float32)
    return 0.75 * diagonal_mask[None] + 0.2 * noise_part / jnp.sqrt(jnp.float32(ARM))


def draw_tile_ids(key, part):
    key_list = jax.random.split(jax.random.fold_in(key, 21), RANKS)

    def one_device(device_key):
        return jax.random.permutation(device_key, NTILE)[:MAXT]
    return jax.vmap(one_device)(key_list).astype(jnp.int32)


def draw_tile_count(key, part):
    heavy_count = MAXT - jax.random.randint(jax.random.fold_in(key, 31), (N_GZ, HALF_XY), 0, MAXT // 4 + 1)
    heavy_count = heavy_count.at[0, 0].set(MAXT)
    light_count = jax.random.randint(jax.random.fold_in(key, 32), (N_GZ, HALF_XY), 0, MAXT - heavy_count + 1)
    heavy_side = jax.random.randint(jax.random.fold_in(key, 33), (N_GZ, HALF_XY), 0, 2)
    first_half = jnp.where(heavy_side == 1, heavy_count, light_count)
    second_half = jnp.where(heavy_side == 1, light_count, heavy_count)
    return jnp.concatenate([first_half, second_half], axis=1).reshape(RANKS).astype(jnp.int32)


def block_levels(own_key, dims, shards, low, high):
    loudness, own = 1.0, jax.random.fold_in(own_key, 6)
    for dim, blocks in shards:
        heights = jnp.exp(jax.random.uniform(jax.random.fold_in(own, dim), (blocks,), jnp.float32, low / len(shards), high / len(shards)))
        loudness = loudness * jnp.repeat(heights, dims[dim] // blocks).reshape([-1 if axis == dim else 1 for axis in range(len(dims))])
    return loudness


def bell_draw(stream_key, dims, width, limit, shards=(), held_as=jnp.bfloat16):
    array = width * jax.random.normal(stream_key, dims, jnp.float32)
    if shards:
        array = array * block_levels(stream_key, dims, shards, -0.22, 0.18)
    return jnp.clip(array, -limit, limit).astype(held_as)


def setup_inputs(seed: int = 0) -> dict:
    arg_keys = jax.random.split(jax.random.key(seed), 9)
    fields = draw_fields(jax.random.fold_in(arg_keys[8], 71), 0)
    conductance = jnp.clip(jnp.exp(math.log(10000.0) - 2.3025851 * jax.random.uniform(arg_keys[1], (4, NZ, NX, NY), jnp.float32) ** block_levels(arg_keys[1], (4, NZ, NX, NY), ((1, 32), (2, 16)), -0.2, 0.2)), 1000.0, 10000.0)
    lateral = jnp.clip(jax.random.uniform(arg_keys[2], (4,), jnp.float32, 0.05, 0.24), 0.05, 0.24)
    partition = jnp.clip(jnp.exp(jax.random.uniform(arg_keys[3], (3,), jnp.float32, math.log(0.1), math.log(0.8))), 0.1, 0.8)
    arm_step = draw_arm_step(jax.random.fold_in(arg_keys[8], 71), 0)
    profiles = bell_draw(arg_keys[5], (3, SLOTS, ARM, TILE), 1.0, 6.0, ((1, 512),), jnp.float32)
    tile_ids = draw_tile_ids(jax.random.fold_in(arg_keys[8], 71), 0)
    tile_count = draw_tile_count(jax.random.fold_in(arg_keys[8], 71), 0)
    return {"fields": fields, "conductance": conductance, "lateral": lateral, "partition": partition, "arm_step": arm_step, "profiles": profiles, "tile_ids": tile_ids, "tile_count": tile_count}


def lever_update(cell_values, profile, partition, arm_step):
    solid_frac = 0.9 / (1.0 + jnp.exp(cell_values[3]))
    solute = cell_values[:3]

    def substep(step_at, current):
        fraction = solid_frac * ((step_at + 1).astype(current.dtype) / SUB)
        average = jnp.mean(current, axis=2)
        liquid = (solute - fraction * average) / (1.0 - fraction)
        spread = jnp.einsum("jab,jsbc->jsac", arm_step, current, precision=lax.Precision.HIGHEST)
        return spread.at[:, :, -1, :].add(0.5 * partition[:, None, None] * liquid)

    evolved = lax.fori_loop(0, SUB, substep, profile)
    change = solid_frac * (jnp.mean(evolved, axis=2) - partition[:, None, None] * solute)
    return evolved, change


def thomas_solve(lower_c, middle_c, upper_c, source):
    stacked = tuple(jnp.moveaxis(values, 1, 0) for values in (lower_c, middle_c, upper_c, source))
    start_plane = jnp.zeros_like(stacked[3][0])

    def sweep_down(carry, row_set):
        prev_up, prev_rhs = carry
        low_here, mid_here, up_here, src_here = row_set
        pivot_value = mid_here - low_here * prev_up
        next_up = up_here / pivot_value
        next_rhs = (src_here - low_here * prev_rhs) / pivot_value
        return (next_up, next_rhs), (next_up, next_rhs)

    unused_carry, (coef_up, coef_rhs) = lax.scan(sweep_down, (start_plane, start_plane), stacked)

    def sweep_up(after_value, row_set):
        up_here, rhs_here = row_set
        result_value = rhs_here - up_here * after_value
        return result_value, result_value

    unused_last, solved_planes = lax.scan(sweep_up, start_plane, (coef_up, coef_rhs), reverse=True)
    return jnp.moveaxis(solved_planes, 0, 1)


def reference(fields, conductance, lateral, partition, arm_step, profiles, tile_ids, tile_count):
    padded = jnp.pad(fields, ((0, 0), (0, 0), (1, 1), (1, 1)))
    laplace = padded[:, :, 2:, 1:-1] + padded[:, :, :-2, 1:-1] + padded[:, :, 1:-1, 2:] + padded[:, :, 1:-1, :-2] - 4.0 * fields
    source = fields + lateral[:, None, None, None] * laplace
    upper_g = conductance.at[:, -1].set(0.0)
    lower_g = jnp.concatenate([jnp.zeros_like(conductance[:, :1]), conductance[:, :-1]], axis=1)
    solved = thomas_solve(-lower_g, 1.0 + lower_g + upper_g, -upper_g, source)
    grouped = fields.reshape(4, N_GZ, CZ, N_XY, CX, NY).transpose(1, 3, 0, 2, 4, 5).reshape(RANKS, 4, NTILE, TILE)
    slot_pos = jnp.arange(MAXT)

    def per_rank(rank_at, state):
        prof_out, delta_tiles = state
        rank_index = rank_at.astype(jnp.int32)
        cell_block = lax.dynamic_index_in_dim(grouped, rank_index, 0, keepdims=False)
        tile_rows = lax.dynamic_index_in_dim(tile_ids, rank_index, 0, keepdims=False)
        live_count = lax.dynamic_index_in_dim(tile_count, rank_index, 0, keepdims=False)
        picked = cell_block[:, tile_rows]
        start_slot = (rank_index * MAXT).astype(jnp.int32)
        current = lax.dynamic_slice_in_dim(profiles, start_slot, MAXT, axis=1)
        evolved, change = lever_update(picked, current, partition, arm_step)
        live_slot = slot_pos < live_count
        evolved = jnp.where(live_slot[None, :, None, None], evolved, 0.0)
        change = jnp.where(live_slot[None, :, None], change, 0.0)
        prof_out = lax.dynamic_update_slice_in_dim(prof_out, evolved, start_slot, axis=1)
        rank_delta = jnp.zeros((3, NTILE, TILE), change.dtype).at[:, tile_rows].add(change)
        delta_tiles = lax.dynamic_update_index_in_dim(delta_tiles, rank_delta, rank_index, 0)
        return prof_out, delta_tiles

    initial = (jnp.zeros_like(profiles), jnp.zeros((RANKS, 3, NTILE, TILE), profiles.dtype))
    new_profiles, delta_tiles = lax.fori_loop(0, RANKS, per_rank, initial)
    delta_field = delta_tiles.reshape(N_GZ, N_XY, 3, CZ, CX, NY).transpose(2, 0, 3, 1, 4, 5).reshape(3, NZ, NX, NY)
    new_fields = jnp.concatenate([solved[:3] + delta_field, solved[3:]], axis=0)
    return new_fields, new_profiles
```

```python
import functools

import jax
import jax.numpy as jnp
from jax import lax
from jax.experimental import pallas as pl
from jax.experimental.pallas import tpu as pltpu
from jax.sharding import PartitionSpec as P

F32 = jnp.float32
BF16 = jnp.bfloat16
MESH = pl.DeviceIdType.MESH
HIGH = lax.Precision.HIGHEST
SUB = 16
ARM = 64
SLOTS = 16
DELTAS = (3, -3, 2, -2, 1, -1)

ORDER = {}
BASE = {}
for _delta in (0,) + DELTAS:
    BASE[_delta] = len(ORDER)
    for _i in range(max(0, -_delta), min(4, 4 - _delta)):
        ORDER[(_i, _i + _delta)] = len(ORDER)
COUNT = {d: 4 - abs(d) for d in DELTAS}


def merge_mass(low, high):
    mass = low[2] + high[1]
    inverse = 1.0 / (mass + low[0] + high[0])
    a, b = low[0] * inverse, high[0] * inverse
    return (a * high[0], low[1] + a * mass, high[2] + b * mass), (a, b, inverse)


def merge_rhs(low, high, a, b, inverse):
    rhs = low[1] + high[0]
    return (low[0] + a * rhs, high[1] + b * rhs), rhs * inverse


def split(x):
    high = x.astype(BF16).astype(F32)
    return high, x - high


def dot(x, y, precision=None):
    return jnp.dot(x, y, precision=precision, preferred_element_type=F32)


def kernel(
    n_xy,
    fields, cond, lateral, partition, arm, profiles, ids, ids_row, count,
    out_fields, out_profiles,
    fld, cnd, src, prof, coef, tail,
    halo_s, halo_r,
    pair_cs, pair_rs, blk_c, blk_r, chip_coef,
    l1_cs, l1_rs, l1_cr, l1_rr, sup_coef,
    l2_cs, l2_rs, l2_cr, l2_rr, ret_s, ret_r,
    back_s, back_r, fin, fin_r,
    cells, wsc, gsc, hsc, lhs1, lhs2, ysc, ssc, change, delta,
    in_sem, prof_sem, out_sem, pout_sem,
    send_sem, recv_sem,
):
    gz = lax.axis_index("gz")
    xy = lax.axis_index("xy")
    core = lax.rem(gz, 2)
    chip = gz // 2
    other = 1 - core
    ring = chip // 4
    phase = lax.rem(chip, 4)

    def at_chip(offset):
        return (lax.rem(chip + (offset + 16), 16) * 2 + core, xy)

    left = (gz, lax.rem(xy + n_xy - 1, n_xy))
    right = (gz, lax.rem(xy + 1, n_xy))
    peer = (chip * 2 + other, xy)

    def load(ref, buf, base, y, sem):
        return pltpu.make_async_copy(
            ref.at[:, pl.ds(128 * y, 128)], buf.at[y + base], in_sem.at[sem + y]
        )

    field_loads = [load(fields, fld, 1, y, 0) for y in range(8)]
    cond_loads = [load(cond, cnd, 0, y, 8) for y in range(8)]
    prof_loads = [
        pltpu.make_async_copy(
            profiles.at[pl.ds(1024 * j, 1024)], prof.at[pl.ds(1024 * j, 1024)], prof_sem.at[j]
        )
        for j in range(3)
    ]
    barrier = pltpu.get_barrier_semaphore()
    partners = [left, right, peer]
    partners += [at_chip(d) for d in DELTAS] + [at_chip(4 * d) for d in (1, 2, 3)]
    for partner in partners:
        pl.semaphore_signal(barrier, inc=1, device_id=partner, device_id_type=MESH)
    for copy in field_loads + cond_loads + prof_loads:
        copy.start()

    sends = []
    used = [0]

    def remote(source, target, device):
        n = used[0]
        used[0] = n + 1
        copy = pltpu.make_async_remote_copy(
            src_ref=source, dst_ref=target, send_sem=send_sem.at[n], recv_sem=recv_sem.at[n],
            device_id=device, device_id_type=MESH,
        )
        copy.start()
        sends.append(copy)
        return copy

    fld[0] = jnp.zeros((128, 128), F32)
    fld[9] = jnp.zeros((128, 128), F32)
    for copy in field_loads:
        copy.wait()
    for y in range(8):
        halo_s[0, y] = fld[y + 1, pl.ds(0, 16, stride=8), :]
        halo_s[1, y] = fld[y + 1, pl.ds(7, 16, stride=8), :]
    pl.semaphore_wait(barrier, len(partners))
    halo = [
        remote(halo_s.at[0], halo_r.at[1], left),
        remote(halo_s.at[1], halo_r.at[0], right),
    ]

    keep = jnp.where(gz == lax.axis_size("gz") - 1, 0.0, 1.0).astype(F32)
    for copy in cond_loads:
        copy.wait()

    def plane(buf, y, f, z):
        return buf[y, pl.ds(pl.multiple_of(f * 32 + z * 8, 8), 8), :]

    def eliminate_mass(owner, p):
        f, y = owner * 2 + p // 8, lax.rem(p, 8)
        e = owner * 16 + p
        block = (plane(cnd, y, f, 0), 1.0, 0.0)
        for z in (1, 2, 3):
            face = plane(cnd, y, f, z)
            if z == 3:
                face = face * keep
            block, held = merge_mass(block, (face, 1.0, 0.0))
            for n in range(3):
                coef[e, 3 * z - 3 + n] = held[n]
        return block

    @pl.loop(0, 16, unroll=4)
    def _(p):
        block = eliminate_mass(other, p)
        for n in range(3):
            pair_cs[p, n] = block[n]

    pair_c = remote(pair_cs, blk_c.at[core], peer)

    @pl.loop(0, 16, unroll=4)
    def _(p):
        block = eliminate_mass(core, p)
        for n in range(3):
            blk_c[core, p, n] = block[n]

    row = lax.broadcasted_iota(jnp.int32, (8, 128), 0)
    lane = lax.broadcasted_iota(jnp.int32, (8, 128), 1)

    @pl.loop(0, 16)
    def _(q):
        at = pl.ds(pl.multiple_of(q * 8, 8), 8)
        rate = lateral[q // 4]
        tiles = [fld[y, at, :] for y in range(10)]
        for y in range(8):
            before, here, after = tiles[y : y + 3]
            down = jnp.where(row == 0, 0.0, pltpu.roll(here, 1, 0))
            up = jnp.where(row == 7, 0.0, pltpu.roll(here, 7, 0))
            low = pltpu.roll(jnp.where(lane == 127, before, here), 1, 1)
            high = pltpu.roll(jnp.where(lane == 0, after, here), 127, 1)
            src[y, at, :] = here + rate * (down + up + low + high - 4.0 * here)

    def powers(j):
        power = arm[j]
        wsc[j] = jnp.full((32, ARM), 1.0 / ARM, F32)
        last = lax.broadcasted_iota(jnp.int32, (ARM, SUB), 0) == ARM - 1
        gsc[j] = jnp.where(last, 1.0, 0.0).astype(F32)
        n = 1
        while n < SUB:
            both = dot(jnp.concatenate([power, wsc[j, 0:8]], axis=0), power, HIGH)
            tips = dot(power, gsc[j], HIGH)
            wsc[j, n : 2 * n] = both[ARM : ARM + n]
            gsc[j, :, n : 2 * n] = tips[:, 0:n]
            power = both[:ARM]
            n *= 2
        wsc[j, SUB : SUB + 1] = jnp.sum(power, axis=0, keepdims=True) * (1.0 / ARM)
        rows = wsc[j]
        end = lax.broadcasted_iota(jnp.int32, (SUB, ARM), 1) == ARM - 1
        held = jnp.sum(jnp.where(end, rows[:SUB], 0.0), axis=1, keepdims=True)
        hsc[j] = jnp.broadcast_to(held, (SUB, 128))
        for n, part in enumerate(split(rows)):
            lhs1[j, :, 128 * n : 128 * n + 64] = part
            lhs1[j, :, 128 * n + 64 : 128 * n + 128] = part
        high, low = split(power)
        lhs2[j, :, 0:64] = high
        lhs2[j, :, 64:128] = high
        lhs2[j, :, 128:192] = low
        high, low = split(gsc[j])
        lhs2[j, :, 192:208] = high
        lhs2[j, :, 208:224] = high
        lhs2[j, :, 224:240] = low
        lhs2[j, :, 240:256] = low

    for j in range(3):
        powers(j)

    for copy in halo:
        copy.wait_recv()
    first = jnp.where(xy == 0, 0.0, 1.0).astype(F32)
    final = jnp.where(xy == n_xy - 1, 0.0, 1.0).astype(F32)

    def eliminate_rhs(owner, p):
        f, y = owner * 2 + p // 8, lax.rem(p, 8)
        e = owner * 16 + p
        rate = lateral[f]
        block = None
        for z in range(4):
            edge = jnp.where(row == 0, halo_r[0, y, pl.ds(f * 4 + z, 1), :] * (rate * first), 0.0)
            edge += jnp.where(row == 7, halo_r[1, y, pl.ds(f * 4 + z, 1), :] * (rate * final), 0.0)
            here = plane(src, y, f, z) + edge
            if z == 0:
                block = (here, 0.0)
            else:
                block, tail[e, z - 1] = merge_rhs(
                    block, (here, 0.0), *(coef[e, 3 * z - 3 + n] for n in range(3))
                )
        return block

    @pl.loop(0, 16, unroll=4)
    def _(p):
        block = eliminate_rhs(other, p)
        for n in range(2):
            pair_rs[p, n] = block[n]

    pair_r = remote(pair_rs, blk_r.at[core], peer)

    @pl.loop(0, 16, unroll=4)
    def _(p):
        block = eliminate_rhs(core, p)
        for n in range(2):
            blk_r[core, p, n] = block[n]

    def part_of(i, m):
        return lax.rem(phase + 4 - i, 4) * 4 + m

    pair_c.wait_recv()
    for (i, m), s in ORDER.items():
        p = part_of(i, m)
        merged, held = merge_mass(*([blk_c[c, p, n] for n in range(3)] for c in range(2)))
        target = l1_cr if i == m else l1_cs
        for n in range(3):
            chip_coef[s, n] = held[n]
            target[s, n] = merged[n]

    def spread(source, target, sign):
        return [
            remote(
                source.at[pl.ds(BASE[d], COUNT[d])], target.at[pl.ds(BASE[d], COUNT[d])],
                at_chip(sign * d),
            )
            for d in DELTAS
        ]

    l1_c = spread(l1_cs, l1_cr, 1)
    pair_r.wait_recv()
    for (i, m), s in ORDER.items():
        p = part_of(i, m)
        merged, ratio = merge_rhs(
            *([blk_r[c, p, n] for n in range(2)] for c in range(2)),
            *(chip_coef[s, n] for n in range(3)),
        )
        chip_coef[s, 2] = ratio
        target = l1_rr if i == m else l1_rs
        for n in range(2):
            target[s, n] = merged[n]
    l1_r = spread(l1_rs, l1_rr, 1)

    for copy in prof_loads:
        copy.wait()

    def tile_pair(j, t):
        at = [pl.multiple_of(j * 1024 + t * 128 + 64 * n, 64) for n in range(2)]
        return at, jnp.concatenate([prof[pl.ds(a, 64), :] for a in at], axis=1)

    @pl.loop(0, 8)
    def _(t):
        for j in range(3):
            unused, tile = tile_pair(j, t)
            high, low = (part.astype(BF16) for part in split(tile))
            means = dot(lhs1[j].astype(BF16), jnp.concatenate([high, low, high, low], axis=0))
            for n in range(2):
                ysc[j, pl.ds(pl.multiple_of(t * 64 + 32 * n, 32), 32), :] = means[:, 128 * n : 128 * n + 128]

    for slot in range(SLOTS):
        tile = ids[0, slot]
        y, at = lax.rem(tile, 8), (tile // 64) * 8 + lax.rem(tile // 8, 8)
        for f in range(4):
            cells[f, slot : slot + 1] = fld[y + 1, pl.ds(f * 32 + at, 1), :]

    def group(buf, m, n_values):
        return [[buf[ORDER[(i, m)], n] for n in range(n_values)] for i in range(4)]

    def slot_of(m):
        return lax.rem(m + 4 - ring, 4)

    for copy in l1_c:
        copy.wait_recv()
    for m in range(4):
        blocks = group(l1_cr, m, 3)
        low, held1 = merge_mass(blocks[0], blocks[1])
        high, held3 = merge_mass(blocks[2], blocks[3])
        merged, held2 = merge_mass(low, high)
        for k, held in enumerate((held1, held2, held3)):
            for n in range(3):
                sup_coef[m, k, n] = held[n]
        for n in range(3):
            l2_cs[slot_of(m), n] = merged[n]
    l2_c = [remote(l2_cs.at[d], l2_cr.at[4 - d], at_chip(4 * d)) for d in (2, 1, 3)]
    for copy in l1_r:
        copy.wait_recv()
    for m in range(4):
        blocks = group(l1_rr, m, 2)
        held = [[sup_coef[m, k, n] for n in range(3)] for k in range(3)]
        low, ratio1 = merge_rhs(blocks[0], blocks[1], *held[0])
        high, ratio3 = merge_rhs(blocks[2], blocks[3], *held[2])
        merged, ratio2 = merge_rhs(low, high, *held[1])
        for k, ratio in enumerate((ratio1, ratio2, ratio3)):
            sup_coef[m, k, 2] = ratio
        for n in range(2):
            l2_rs[slot_of(m), n] = merged[n]
    l2_r = [remote(l2_rs.at[d], l2_rr.at[4 - d], at_chip(4 * d)) for d in (2, 1, 3)]

    live = lax.broadcasted_iota(jnp.int32, (SLOTS, 128), 0) < count[0]
    solid = 0.9 / (1.0 + jnp.exp(cells[3]))
    inverses = [1.0 / (1.0 - solid * ((k + 1) / SUB)) for k in range(SUB)]
    for j in range(3):
        solute = cells[j]
        half = 0.5 * partition[j]
        liquids = []
        for k in range(SUB + 1):
            mean = ysc[j, pl.ds(k, SLOTS, stride=32), :]
            for i in range(k):
                mean += hsc[j, k - 1 - i : k - i, :] * liquids[i]
            if k == SUB:
                moved = solid * (mean - partition[j] * solute)
                change[:, 128 * j : 128 * j + 128] = jnp.where(live, moved, 0.0)
            else:
                fraction = solid * ((k + 1) / SUB)
                liquids.append(half * ((solute - fraction * mean) * inverses[k]))
                ssc[j, pl.ds(SUB - 1 - k, SLOTS, stride=SUB), :] = liquids[k]

    for copy in l2_c:
        copy.wait_recv()
    masses = [[(l2_cr if b else l2_cs)[b, n] for n in range(3)] for b in range(4)]
    low, held1 = merge_mass(masses[0], masses[1])
    high, held3 = merge_mass(masses[2], masses[3])
    whole, held2 = merge_mass(low, high)
    for copy in l2_r:
        copy.wait_recv()
    rhs = [[(l2_rr if b else l2_rs)[b, n] for n in range(2)] for b in range(4)]
    low, ratio1 = merge_rhs(rhs[0], rhs[1], *held1)
    high, ratio3 = merge_rhs(rhs[2], rhs[3], *held3)
    total, ratio2 = merge_rhs(low, high, *held2)
    v0 = (total[0] + total[1]) / (whole[1] + whole[2])
    v2 = ratio2 + (held2[0] + held2[1]) * v0
    v1 = ratio1 + held1[0] * v0 + held1[1] * v2
    v3 = ratio3 + held3[0] * v2 + held3[1] * v0
    values = [v0, v1, v2, v3, v0]
    for b in range(4):
        target = ret_s if b else ret_r
        target[b, 0] = values[b]
        target[b, 1] = values[b + 1]
    ret = [remote(ret_s.at[b], ret_r.at[4 - b], at_chip(4 * b)) for b in (2, 1, 3)]

    def evolve(j):
        @pl.loop(0, 8)
        def _(t):
            at, tile = tile_pair(j, t)
            tips = jnp.concatenate(
                [ssc[j, pl.ds(pl.multiple_of(t * 32 + 16 * n, 16), 16), :] for n in range(2)], axis=1
            )
            high, low = (part.astype(BF16) for part in split(tile))
            tip_high, tip_low = (part.astype(BF16) for part in split(tips))
            evolved = dot(
                lhs2[j].astype(BF16),
                jnp.concatenate(
                    [high, low, high, tip_high, tip_low, tip_high, tip_low], axis=0
                ),
            )
            for n in range(2):
                shown = jnp.full((ARM, 128), 2 * t + n, jnp.int32) < count[0]
                prof[pl.ds(at[n], 64), :] = jnp.where(
                    shown, evolved[:, 128 * n : 128 * n + 128], 0.0
                )

        copy = pltpu.make_async_copy(
            prof.at[pl.ds(1024 * j, 1024)], out_profiles.at[pl.ds(1024 * j, 1024)], pout_sem.at[j]
        )
        copy.start()
        return copy

    stores = [evolve(0)]

    for copy in ret:
        copy.wait_recv()
    for m in range(4):
        s = slot_of(m)
        x0, x4 = ret_r[s, 0], ret_r[s, 1]
        held = [[sup_coef[m, k, n] for n in range(3)] for k in range(3)]
        x2 = held[1][2] + held[1][0] * x0 + held[1][1] * x4
        x1 = held[0][2] + held[0][0] * x0 + held[0][1] * x2
        x3 = held[2][2] + held[2][0] * x2 + held[2][1] * x4
        values = [x0, x1, x2, x3, x4]
        for i in range(4):
            target = back_r if i == m else back_s
            for n in range(2):
                target[ORDER[(i, m)], n] = values[i + n]
    back = spread(back_s, back_r, -1)

    stores.append(evolve(1))
    stores.append(evolve(2))

    place = lax.broadcasted_iota(jnp.int32, (256, SLOTS), 0)
    named = (place // 64) * 64 + lax.rem(place, 8) * 8 + lax.rem(place // 8, 8)
    hit = jnp.where(named == ids_row[...], 1.0, 0.0).astype(BF16)
    rest = change[...]
    spreads = None
    for n in range(3):
        piece = rest.astype(BF16)
        rest = rest - piece.astype(F32)
        term = dot(hit, piece)
        spreads = term if spreads is None else spreads + term
    for j in range(3):
        delta[j] = spreads[:, 128 * j : 128 * j + 128]
    delta[3] = jnp.zeros((256, 128), F32)

    for copy in back:
        copy.wait_recv()
    for (i, m), s in ORDER.items():
        p = part_of(i, m)
        low, high = back_r[s, 0], back_r[s, 1]
        middle = chip_coef[s, 2] + chip_coef[s, 0] * low + chip_coef[s, 1] * high
        fin[0, p, 0] = low
        fin[0, p, 1] = middle
        fin[1, p, 0] = middle
        fin[1, p, 1] = high
    last = remote(fin.at[other], fin_r, peer)

    def finish(owner, p, low, high):
        f, y = owner * 2 + p // 8, lax.rem(p, 8)
        e = owner * 16 + p
        above = high
        values = [low, None, None, None]
        for z in (3, 2, 1):
            above = tail[e, z - 1] + coef[e, 3 * z - 3] * low + coef[e, 3 * z - 2] * above
            values[z] = above
        for z in range(4):
            at = pl.ds(pl.multiple_of(f * 32 + z * 8, 8), 8)
            src[y, at, :] = values[z] + delta[f, pl.ds(pl.multiple_of(z * 64 + y * 8, 8), 8), :]

    def store(owner, n):
        for y in range(8):
            rows = pl.ds(pl.multiple_of(owner * 64, 64), 64)
            copy = pltpu.make_async_copy(
                src.at[y, rows], out_fields.at[rows, pl.ds(128 * y, 128)], out_sem.at[n + y]
            )
            copy.start()
            stores.append(copy)

    @pl.loop(0, 16, unroll=4)
    def _(p):
        finish(core, p, fin[core, p, 0], fin[core, p, 1])

    store(core, 0)
    last.wait_recv()

    @pl.loop(0, 16, unroll=4)
    def _(p):
        finish(other, p, fin_r[p, 0], fin_r[p, 1])

    store(other, 8)
    for copy in sends:
        copy.wait_send()
    for copy in stores:
        copy.wait()


def body(fields, conductance, lateral, partition, arm_step, profiles, tile_ids, tile_count):
    tile = (8, 128)
    scratch = [
        (10, 128, 128), (8, 128, 128), (8, 128, 128), (3072, 128), (32, 9) + tile, (32, 3) + tile,
        (2, 8, 16, 128), (2, 8, 16, 128),
        (16, 3) + tile, (16, 2) + tile, (2, 16, 3) + tile, (2, 16, 2) + tile, (16, 3) + tile,
        (16, 3) + tile, (16, 2) + tile, (16, 3) + tile, (16, 2) + tile, (4, 3, 3) + tile,
        (4, 3) + tile, (4, 2) + tile, (4, 3) + tile, (4, 2) + tile, (4, 2) + tile, (4, 2) + tile,
        (16, 2) + tile, (16, 2) + tile, (2, 16, 2) + tile, (16, 2) + tile,
        (4, 16, 128), (3, 32, 64), (3, 64, 16), (3, 16, 128), (3, 32, 256), (3, 64, 256),
        (3, 512, 128), (3, 256, 128), (16, 384), (4, 256, 128),
    ]
    smem = pl.BlockSpec(memory_space=pltpu.SMEM)
    vmem = pl.BlockSpec(memory_space=pltpu.VMEM)
    hbm = pl.BlockSpec(memory_space=pl.ANY)
    new_fields, new_profiles = pl.pallas_call(
        functools.partial(kernel, lax.axis_size("xy")),
        out_shape=(
            jax.ShapeDtypeStruct((128, 1024), F32),
            jax.ShapeDtypeStruct((3072, 128), F32),
        ),
        in_specs=[hbm, hbm, smem, smem, vmem, hbm, smem, vmem, smem],
        out_specs=(hbm, hbm),
        scratch_shapes=[pltpu.VMEM(shape, F32) for shape in scratch]
        + [
            pltpu.SemaphoreType.DMA((16,)),
            pltpu.SemaphoreType.DMA((3,)),
            pltpu.SemaphoreType.DMA((16,)),
            pltpu.SemaphoreType.DMA((3,)),
            pltpu.SemaphoreType.DMA((32,)),
            pltpu.SemaphoreType.DMA((32,)),
        ],
        compiler_params=pltpu.CompilerParams(
            collective_id=0, has_side_effects=True, vmem_limit_bytes=40 * 2**20
        ),
        cost_estimate=pl.CostEstimate(flops=10**9, bytes_accessed=5 * 2**20, transcendentals=2048),
        name="ingot",
    )(
        fields.reshape(128, 1024), conductance.reshape(128, 1024), lateral, partition, arm_step,
        profiles.reshape(3072, 128), tile_ids, tile_ids, tile_count,
    )
    return new_fields.reshape(fields.shape), new_profiles.reshape(profiles.shape)


def solution(mesh):
    return jax.shard_map(
        body,
        mesh=mesh,
        in_specs=(
            P(None, "gz", "xy", None),
            P(None, "gz", "xy", None),
            P(),
            P(),
            P(),
            P(None, ("gz", "xy"), None, None),
            P(("gz", "xy"), None),
            P(("gz", "xy")),
        ),
        out_specs=(P(None, "gz", "xy", None), P(None, ("gz", "xy"), None, None)),
        check_vma=False,
    )
```

```python
import functools

import jax
import jax.numpy as jnp
from jax import lax
from jax.experimental import pallas as pl
from jax.experimental.pallas import tpu as pltpu
from jax.sharding import PartitionSpec as P

F32 = jnp.float32
BF16 = jnp.bfloat16
MESH = pl.DeviceIdType.MESH
HIGH = lax.Precision.HIGHEST
SUB = 16
ARM = 64
SLOTS = 16
CHIPS = 16
OFFSETS = (8, 7, 9, 6, 10, 5, 11, 4, 12, 3, 13, 2, 14, 1, 15)


def merge_mass(low, high):
    mass = low[2] + high[1]
    inverse = 1.0 / (mass + low[0] + high[0])
    a, b = low[0] * inverse, high[0] * inverse
    return (a * high[0], low[1] + a * mass, high[2] + b * mass), (a, b, inverse)


def merge_rhs(low, high, a, b, inverse):
    rhs = low[1] + high[0]
    return (low[0] + a * rhs, high[1] + b * rhs), rhs * inverse


def split(x):
    high = x.astype(BF16).astype(F32)
    return high, x - high


def dot(x, y, precision=None):
    return jnp.dot(x, y, precision=precision, preferred_element_type=F32)


def kernel(
    n_xy,
    fields, cond, lateral_in, partition_in, arm_in, profiles, ids_in, count,
    out_fields, out_profiles,
    lateral, partition, ids, ids_row, arm,
    fld, cnd, src, prof, coef, tail,
    halo_s, halo_r,
    pair_cs, pair_rs, blk_c, blk_r, chip_coef,
    ring_cs, ring_rs, ring_cr, ring_rr, ret_s, ret_r, fin, fin_r, top_coef,
    cells, wsc, gsc, hsc, lhs1, lhs2, ysc, ssc, change, delta,
    in_sem, small_sem, prof_sem,
    send_sem, recv_sem,
):
    gz = lax.axis_index("gz")
    xy = lax.axis_index("xy")
    core = lax.rem(gz, 2)
    chip = gz // 2
    other = 1 - core

    def at_chip(offset):
        return (lax.rem(chip + offset, CHIPS) * 2 + core, xy)

    left = (gz, lax.rem(xy + n_xy - 1, n_xy))
    right = (gz, lax.rem(xy + 1, n_xy))
    peer = (chip * 2 + other, xy)

    def load(ref, buf, base, y, sem):
        return pltpu.make_async_copy(
            ref.at[:, pl.ds(128 * y, 128)], buf.at[y + base], in_sem.at[sem + y]
        )

    field_loads = [load(fields, fld, 1, y, 0) for y in range(8)]
    cond_loads = [load(cond, cnd, 0, y, 8) for y in range(8)]
    prof_loads = [
        pltpu.make_async_copy(
            profiles.at[pl.ds(1024 * j, 1024)], prof.at[pl.ds(1024 * j, 1024)], prof_sem.at[j]
        )
        for j in range(3)
    ]
    small = [(lateral_in, lateral), (partition_in, partition), (ids_in, ids)]
    small += [(ids_in, ids_row), (arm_in, arm)]
    small_loads = [
        pltpu.make_async_copy(ref, buf, small_sem.at[n]) for n, (ref, buf) in enumerate(small)
    ]
    barrier = pltpu.get_barrier_semaphore()
    partners = [left, right, peer]
    partners += [at_chip(d) for d in OFFSETS]
    for partner in partners:
        pl.semaphore_signal(barrier, inc=1, device_id=partner, device_id_type=MESH)
    for copy in field_loads + cond_loads + small_loads + prof_loads:
        copy.start()

    sends = []
    used = [0]

    def remote(source, target, device):
        n = used[0]
        used[0] = n + 1
        copy = pltpu.make_async_remote_copy(
            src_ref=source, dst_ref=target, send_sem=send_sem.at[n], recv_sem=recv_sem.at[n],
            device_id=device, device_id_type=MESH,
        )
        copy.start()
        sends.append(copy)
        return copy

    fld[0] = jnp.zeros((128, 128), F32)
    fld[9] = jnp.zeros((128, 128), F32)
    for copy in field_loads:
        copy.wait()
    for y in range(8):
        halo_s[0, y] = fld[y + 1, pl.ds(0, 16, stride=8), :]
        halo_s[1, y] = fld[y + 1, pl.ds(7, 16, stride=8), :]
    keep = jnp.where(gz == lax.axis_size("gz") - 1, 0.0, 1.0).astype(F32)
    for copy in cond_loads:
        copy.wait()

    def plane(buf, y, f, z):
        return buf[y, pl.ds(pl.multiple_of(f * 32 + z * 8, 8), 8), :]

    def eliminate_mass(owner, p):
        f, y = owner * 2 + p // 8, lax.rem(p, 8)
        e = owner * 16 + p
        block = (plane(cnd, y, f, 0), 1.0, 0.0)
        for z in (1, 2, 3):
            face = plane(cnd, y, f, z)
            if z == 3:
                face = face * keep
            block, held = merge_mass(block, (face, 1.0, 0.0))
            for n in range(3):
                coef[e, 3 * z - 3 + n] = held[n]
        return block

    @pl.loop(0, 16, unroll=4)
    def _(p):
        block = eliminate_mass(other, p)
        for n in range(3):
            pair_cs[p, n] = block[n]

    pl.semaphore_wait(barrier, len(partners))
    halo = [
        remote(halo_s.at[0], halo_r.at[1], left),
        remote(halo_s.at[1], halo_r.at[0], right),
    ]
    pair_c = remote(pair_cs, blk_c.at[core], peer)

    @pl.loop(0, 16, unroll=4)
    def _(p):
        block = eliminate_mass(core, p)
        for n in range(3):
            blk_c[core, p, n] = block[n]

    for copy in small_loads:
        copy.wait()
    row = lax.broadcasted_iota(jnp.int32, (8, 128), 0)
    lane = lax.broadcasted_iota(jnp.int32, (8, 128), 1)

    @pl.loop(0, 16)
    def _(q):
        at = pl.ds(pl.multiple_of(q * 8, 8), 8)
        rate = lateral[q // 4]
        tiles = [fld[y, at, :] for y in range(10)]
        for y in range(8):
            before, here, after = tiles[y : y + 3]
            down = jnp.where(row == 0, 0.0, pltpu.roll(here, 1, 0))
            up = jnp.where(row == 7, 0.0, pltpu.roll(here, 7, 0))
            low = pltpu.roll(jnp.where(lane == 127, before, here), 1, 1)
            high = pltpu.roll(jnp.where(lane == 0, after, here), 127, 1)
            src[y, at, :] = here + rate * (down + up + low + high - 4.0 * here)

    def powers(j):
        power = arm[j]
        wsc[j] = jnp.full((32, ARM), 1.0 / ARM, F32)
        last = lax.broadcasted_iota(jnp.int32, (ARM, SUB), 0) == ARM - 1
        gsc[j] = jnp.where(last, 1.0, 0.0).astype(F32)
        n = 1
        while n < SUB:
            both = dot(jnp.concatenate([power, wsc[j, 0:8]], axis=0), power, HIGH)
            tips = dot(power, gsc[j], HIGH)
            wsc[j, n : 2 * n] = both[ARM : ARM + n]
            gsc[j, :, n : 2 * n] = tips[:, 0:n]
            power = both[:ARM]
            n *= 2
        wsc[j, SUB : SUB + 1] = jnp.sum(power, axis=0, keepdims=True) * (1.0 / ARM)
        rows = wsc[j]
        end = lax.broadcasted_iota(jnp.int32, (SUB, ARM), 1) == ARM - 1
        held = jnp.sum(jnp.where(end, rows[:SUB], 0.0), axis=1, keepdims=True)
        hsc[j] = jnp.broadcast_to(held, (SUB, 128))
        for n, part in enumerate(split(rows)):
            lhs1[j, :, 128 * n : 128 * n + 64] = part
            lhs1[j, :, 128 * n + 64 : 128 * n + 128] = part
        high, low = split(power)
        lhs2[j, :, 0:64] = high
        lhs2[j, :, 64:128] = high
        lhs2[j, :, 128:192] = low
        high, low = split(gsc[j])
        lhs2[j, :, 192:208] = high
        lhs2[j, :, 208:224] = high
        lhs2[j, :, 224:240] = low
        lhs2[j, :, 240:256] = low

    pair_c.wait_recv()
    for d in range(CHIPS):
        p = lax.rem(chip + d, CHIPS)
        merged, held = merge_mass(*([blk_c[c, p, n] for n in range(3)] for c in range(2)))
        for n in range(3):
            chip_coef[d, n] = held[n]
            ring_cs[d, n] = merged[n]
    ring_c = [remote(ring_cs.at[d], ring_cr.at[CHIPS - d], at_chip(d)) for d in OFFSETS]

    for copy in halo:
        copy.wait_recv()
    first = jnp.where(xy == 0, 0.0, 1.0).astype(F32)
    final = jnp.where(xy == n_xy - 1, 0.0, 1.0).astype(F32)

    def eliminate_rhs(owner, p):
        f, y = owner * 2 + p // 8, lax.rem(p, 8)
        e = owner * 16 + p
        rate = lateral[f]
        block = None
        for z in range(4):
            edge = jnp.where(row == 0, halo_r[0, y, pl.ds(f * 4 + z, 1), :] * (rate * first), 0.0)
            edge += jnp.where(row == 7, halo_r[1, y, pl.ds(f * 4 + z, 1), :] * (rate * final), 0.0)
            here = plane(src, y, f, z) + edge
            if z == 0:
                block = (here, 0.0)
            else:
                block, tail[e, z - 1] = merge_rhs(
                    block, (here, 0.0), *(coef[e, 3 * z - 3 + n] for n in range(3))
                )
        return block

    @pl.loop(0, 16, unroll=4)
    def _(p):
        block = eliminate_rhs(other, p)
        for n in range(2):
            pair_rs[p, n] = block[n]

    pair_r = remote(pair_rs, blk_r.at[core], peer)

    @pl.loop(0, 16, unroll=4)
    def _(p):
        block = eliminate_rhs(core, p)
        for n in range(2):
            blk_r[core, p, n] = block[n]

    pair_r.wait_recv()
    for d in range(CHIPS):
        p = lax.rem(chip + d, CHIPS)
        merged, chip_coef[d, 2] = merge_rhs(
            *([blk_r[c, p, n] for n in range(2)] for c in range(2)),
            *(chip_coef[d, n] for n in range(3)),
        )
        for n in range(2):
            ring_rs[d, n] = merged[n]
    ring_r = [remote(ring_rs.at[d], ring_rr.at[CHIPS - d], at_chip(d)) for d in OFFSETS]

    for j in range(3):
        powers(j)


    for copy in prof_loads:
        copy.wait()

    def tile_pair(j, t):
        at = [pl.multiple_of(j * 1024 + t * 128 + 64 * n, 64) for n in range(2)]
        return at, jnp.concatenate([prof[pl.ds(a, 64), :] for a in at], axis=1)

    @pl.loop(0, 8)
    def _(t):
        for j in range(3):
            unused, tile = tile_pair(j, t)
            high, low = (part.astype(BF16) for part in split(tile))
            means = dot(lhs1[j].astype(BF16), jnp.concatenate([high, low, high, low], axis=0))
            for n in range(2):
                ysc[j, pl.ds(pl.multiple_of(t * 64 + 32 * n, 32), 32), :] = means[:, 128 * n : 128 * n + 128]

    for slot in range(SLOTS):
        tile = ids[0, slot]
        y, at = lax.rem(tile, 8), (tile // 64) * 8 + lax.rem(tile // 8, 8)
        for f in range(4):
            cells[f, slot : slot + 1] = fld[y + 1, pl.ds(f * 32 + at, 1), :]

    live = lax.broadcasted_iota(jnp.int32, (SLOTS, 128), 0) < count[0]
    solid = 0.9 / (1.0 + jnp.exp(cells[3]))
    inverses = [1.0 / (1.0 - solid * ((k + 1) / SUB)) for k in range(SUB)]
    for j in range(3):
        solute = cells[j]
        half = 0.5 * partition[j]
        liquids = []
        for k in range(SUB + 1):
            mean = ysc[j, pl.ds(k, SLOTS, stride=32), :]
            for i in range(k):
                mean += hsc[j, k - 1 - i : k - i, :] * liquids[i]
            if k == SUB:
                moved = solid * (mean - partition[j] * solute)
                change[:, 128 * j : 128 * j + 128] = jnp.where(live, moved, 0.0)
            else:
                fraction = solid * ((k + 1) / SUB)
                liquids.append(half * ((solute - fraction * mean) * inverses[k]))
                ssc[j, pl.ds(SUB - 1 - k, SLOTS, stride=SUB), :] = liquids[k]

    for copy in ring_c:
        copy.wait_recv()
    masses = [[(ring_cr if b else ring_cs)[b, n] for n in range(3)] for b in range(CHIPS)]
    levels = []
    while len(masses) > 1:
        joined = [merge_mass(*masses[b : b + 2]) for b in range(0, len(masses), 2)]
        masses = [block for block, held in joined]
        levels.append([held for block, held in joined])
    for n, held in enumerate(held for level in levels for held in level):
        for k in range(3):
            top_coef[n, k] = held[k]
    top_mass = masses[0][1] + masses[0][2]

    for copy in ring_r:
        copy.wait_recv()
    rhs = [[(ring_rr if b else ring_rs)[b, n] for n in range(2)] for b in range(CHIPS)]
    levels, n = [], 0
    while len(rhs) > 1:
        level, joined = [], []
        for b in range(0, len(rhs), 2):
            a, c, inverse = (top_coef[n, k] for k in range(3))
            block, ratio = merge_rhs(rhs[b], rhs[b + 1], a, c, inverse)
            joined.append(block)
            level.append((a, c, ratio))
            n += 1
        rhs = joined
        levels.append(level)
    values = [(rhs[0][0] + rhs[0][1]) / top_mass] * 2
    for level in reversed(levels):
        finer = [values[0]]
        for b, (a, c, ratio) in enumerate(level):
            finer += [ratio + a * values[b] + c * values[b + 1], values[b + 1]]
        values = finer
    for b in range(CHIPS):
        target = ret_s if b else ret_r
        for n in range(2):
            target[b, n] = values[b + n]
    ret = [remote(ret_s.at[b], ret_r.at[CHIPS - b], at_chip(b)) for b in OFFSETS]

    def evolve(j):
        @pl.loop(0, 8)
        def _(t):
            at, tile = tile_pair(j, t)
            tips = jnp.concatenate(
                [ssc[j, pl.ds(pl.multiple_of(t * 32 + 16 * n, 16), 16), :] for n in range(2)], axis=1
            )
            high, low = (part.astype(BF16) for part in split(tile))
            tip_high, tip_low = (part.astype(BF16) for part in split(tips))
            evolved = dot(
                lhs2[j].astype(BF16),
                jnp.concatenate(
                    [high, low, high, tip_high, tip_low, tip_high, tip_low], axis=0
                ),
            )
            for n in range(2):
                shown = jnp.full((ARM, 128), 2 * t + n, jnp.int32) < count[0]
                out_profiles[pl.ds(at[n], 64), :] = jnp.where(
                    shown, evolved[:, 128 * n : 128 * n + 128], 0.0
                )

    for j in range(3):
        evolve(j)

    place = lax.broadcasted_iota(jnp.int32, (256, SLOTS), 0)
    named = (place // 64) * 64 + lax.rem(place, 8) * 8 + lax.rem(place // 8, 8)
    hit = jnp.where(named == ids_row[...], 1.0, 0.0).astype(BF16)
    rest = change[...]
    spreads = None
    for n in range(3):
        piece = rest.astype(BF16)
        rest = rest - piece.astype(F32)
        term = dot(hit, piece)
        spreads = term if spreads is None else spreads + term
    for j in range(3):
        delta[j] = spreads[:, 128 * j : 128 * j + 128]
    delta[3] = jnp.zeros((256, 128), F32)

    for copy in ret:
        copy.wait_recv()
    for d in range(CHIPS):
        p = lax.rem(chip + d, CHIPS)
        low, high = ret_r[d, 0], ret_r[d, 1]
        middle = chip_coef[d, 2] + chip_coef[d, 0] * low + chip_coef[d, 1] * high
        fin[0, p, 0] = low
        fin[0, p, 1] = middle
        fin[1, p, 0] = middle
        fin[1, p, 1] = high
    last = remote(fin.at[other], fin_r, peer)

    def finish(owner, p, low, high):
        f, y = owner * 2 + p // 8, lax.rem(p, 8)
        e = owner * 16 + p
        above = high
        values = [low, None, None, None]
        for z in (3, 2, 1):
            above = tail[e, z - 1] + coef[e, 3 * z - 3] * low + coef[e, 3 * z - 2] * above
            values[z] = above
        lanes = pl.ds(pl.multiple_of(y * 128, 128), 128)
        for z in range(4):
            at = pl.ds(pl.multiple_of(f * 32 + z * 8, 8), 8)
            out_fields[at, lanes] = values[z] + delta[f, pl.ds(pl.multiple_of(z * 64 + y * 8, 8), 8), :]

    @pl.loop(0, 16, unroll=4)
    def _(p):
        finish(core, p, fin[core, p, 0], fin[core, p, 1])

    last.wait_recv()

    @pl.loop(0, 16, unroll=4)
    def _(p):
        finish(other, p, fin_r[p, 0], fin_r[p, 1])

    for copy in sends:
        copy.wait_send()


def deliver(new_fields, new_profiles, out_fields, out_profiles, sem):
    copies = [pltpu.make_async_copy(new_fields, out_fields, sem.at[0])]
    for n in range(3):
        rows = pl.ds(1024 * n, 1024)
        copies.append(
            pltpu.make_async_copy(new_profiles.at[rows], out_profiles.at[rows], sem.at[n + 1])
        )
    for copy in copies:
        copy.start()
    for copy in copies:
        copy.wait()


def body(fields, conductance, lateral, partition, arm_step, profiles, tile_ids, tile_count):
    tile = (8, 128)
    scratch = [
        (10, 128, 128), (8, 128, 128), (8, 128, 128), (3072, 128), (32, 9) + tile, (32, 3) + tile,
        (2, 8, 16, 128), (2, 8, 16, 128),
        (16, 3) + tile, (16, 2) + tile, (2, 16, 3) + tile, (2, 16, 2) + tile, (16, 3) + tile,
        (16, 3) + tile, (16, 2) + tile, (16, 3) + tile, (16, 2) + tile, (16, 2) + tile, (16, 2) + tile,
        (2, 16, 2) + tile, (16, 2) + tile, (15, 3) + tile,
        (4, 16, 128), (3, 32, 64), (3, 64, 16), (3, 16, 128), (3, 32, 256), (3, 64, 256),
        (3, 512, 128), (3, 256, 128), (16, 384), (4, 256, 128),
    ]
    hbm = pl.BlockSpec(memory_space=pl.ANY)
    vmem = pl.BlockSpec(memory_space=pltpu.VMEM)
    operands = [
        pltpu.with_memory_space_constraint(x, pltpu.HBM)
        for x in (
            fields.reshape(128, 1024), conductance.reshape(128, 1024), lateral, partition,
            arm_step, profiles.reshape(3072, 128), tile_ids,
        )
    ]
    new_fields, new_profiles = pl.pallas_call(
        functools.partial(kernel, lax.axis_size("xy")),
        out_shape=(pltpu.VMEM((128, 1024), F32), pltpu.VMEM((3072, 128), F32)),
        in_specs=[hbm] * 7 + [pl.BlockSpec(memory_space=pltpu.SMEM)],
        out_specs=(vmem, vmem),
        scratch_shapes=[
            pltpu.SMEM((4,), F32), pltpu.SMEM((3,), F32),
            pltpu.SMEM((1, SLOTS), jnp.int32),
            pltpu.VMEM((1, SLOTS), jnp.int32), pltpu.VMEM((3, ARM, ARM), F32),
        ]
        + [pltpu.VMEM(shape, F32) for shape in scratch]
        + [
            pltpu.SemaphoreType.DMA((16,)),
            pltpu.SemaphoreType.DMA((5,)),
            pltpu.SemaphoreType.DMA((3,)),
            pltpu.SemaphoreType.DMA((50,)),
            pltpu.SemaphoreType.DMA((50,)),
        ],
        compiler_params=pltpu.CompilerParams(
            collective_id=0, has_side_effects=True, vmem_limit_bytes=40 * 2**20
        ),
        cost_estimate=pl.CostEstimate(flops=10**9, bytes_accessed=5 * 2**20, transcendentals=2048),
        name="ingot",
    )(*operands, tile_count)
    new_fields, new_profiles = pl.pallas_call(
        deliver,
        out_shape=(pltpu.HBM((128, 1024), F32), pltpu.HBM((3072, 128), F32)),
        in_specs=[vmem, vmem],
        out_specs=(hbm, hbm),
        scratch_shapes=[pltpu.SemaphoreType.DMA((4,))],
        cost_estimate=pl.CostEstimate(flops=0, bytes_accessed=2**22, transcendentals=0),
        name="deliver",
    )(
        pltpu.with_memory_space_constraint(new_fields, pltpu.VMEM),
        pltpu.with_memory_space_constraint(new_profiles, pltpu.VMEM),
    )
    return new_fields.reshape(fields.shape), new_profiles.reshape(profiles.shape)


def solution(mesh):
    return jax.shard_map(
        body,
        mesh=mesh,
        in_specs=(
            P(None, "gz", "xy", None),
            P(None, "gz", "xy", None),
            P(),
            P(),
            P(),
            P(None, ("gz", "xy"), None, None),
            P(("gz", "xy"), None),
            P(("gz", "xy")),
        ),
        out_specs=(P(None, "gz", "xy", None), P(None, ("gz", "xy"), None, None)),
        check_vma=False,
    )
```

```python
import functools

import jax
import jax.numpy as jnp
from jax import lax
from jax.experimental import pallas as pl
from jax.experimental.pallas import tpu as pltpu
from jax.sharding import PartitionSpec as P

F32 = jnp.float32
BF16 = jnp.bfloat16
MESH = pl.DeviceIdType.MESH
HIGH = lax.Precision.HIGHEST
SUB = 16
ARM = 64
SLOTS = 16
CHIPS = 16
HALF = CHIPS // 2
REACH = 5
TO = [REACH - i for i in range(HALF)] + [2 * REACH - i for i in range(HALF, CHIPS)]
SENT = sorted((i for i in range(CHIPS) if TO[i]), key=lambda i: (-abs(TO[i]), i))


def merge_mass(low, high):
    mass = low[2] + high[1]
    inverse = 1.0 / (mass + low[0] + high[0])
    a, b = low[0] * inverse, high[0] * inverse
    return (a * high[0], low[1] + a * mass, high[2] + b * mass), (a, b, inverse)


def merge_rhs(low, high, a, b, inverse):
    rhs = low[1] + high[0]
    return (low[0] + a * rhs, high[1] + b * rhs), rhs * inverse


def split(x):
    high = x.astype(BF16).astype(F32)
    return high, x - high


def dot(x, y, precision=None):
    return jnp.dot(x, y, precision=precision, preferred_element_type=F32)


def kernel(
    n_xy,
    fields, cond, lateral_in, partition_in, arm_in, profiles, ids_in, count,
    out_fields, out_profiles,
    lateral, partition, ids, ids_row, arm,
    fld, cnd, src, prof, coef, tail,
    halo_s, halo_r,
    pair_cs, pair_rs, blk_c, blk_r, chip_coef,
    ring_cs, ring_rs, ring_cr, ring_rr, half_cs, half_rs, half_cr, half_rr,
    ret_s, ret_r, fin, fin_r, top_coef,
    cells, wsc, gsc, hsc, lhs1, lhs2, ysc, ssc, change, delta,
    in_sem, small_sem, prof_sem,
    send_sem, recv_sem,
):
    gz = lax.axis_index("gz")
    xy = lax.axis_index("xy")
    core = lax.rem(gz, 2)
    chip = gz // 2
    other = 1 - core

    def at_chip(offset):
        return (lax.rem(chip + (offset + CHIPS), CHIPS) * 2 + core, xy)

    left = (gz, lax.rem(xy + n_xy - 1, n_xy))
    right = (gz, lax.rem(xy + 1, n_xy))
    peer = (chip * 2 + other, xy)

    def load(ref, buf, base, y, sem):
        return pltpu.make_async_copy(
            ref.at[:, pl.ds(128 * y, 128)], buf.at[y + base], in_sem.at[sem + y]
        )

    field_loads = [load(fields, fld, 1, y, 0) for y in range(8)]
    cond_loads = [load(cond, cnd, 0, y, 8) for y in range(8)]
    prof_loads = [
        pltpu.make_async_copy(
            profiles.at[pl.ds(1024 * j, 1024)], prof.at[pl.ds(1024 * j, 1024)], prof_sem.at[j]
        )
        for j in range(3)
    ]
    small = [(lateral_in, lateral), (partition_in, partition), (ids_in, ids)]
    small += [(ids_in, ids_row), (arm_in, arm)]
    small_loads = [
        pltpu.make_async_copy(ref, buf, small_sem.at[n]) for n, (ref, buf) in enumerate(small)
    ]
    barrier = pltpu.get_barrier_semaphore()
    has_left, has_right = xy > 0, xy < n_xy - 1

    @pl.when(has_left)
    def _():
        pl.semaphore_signal(barrier, inc=1, device_id=left, device_id_type=MESH)

    @pl.when(has_right)
    def _():
        pl.semaphore_signal(barrier, inc=1, device_id=right, device_id_type=MESH)

    partners = [peer] + [at_chip(d * sign) for d in range(1, REACH + 1) for sign in (1, -1)]
    for partner in partners:
        pl.semaphore_signal(barrier, inc=1, device_id=partner, device_id_type=MESH)
    for copy in field_loads + cond_loads + small_loads + prof_loads:
        copy.start()

    sends = []
    used = [0]

    def describe(source, target, device):
        n = used[0]
        used[0] = n + 1
        return pltpu.make_async_remote_copy(
            src_ref=source, dst_ref=target, send_sem=send_sem.at[n], recv_sem=recv_sem.at[n],
            device_id=device, device_id_type=MESH,
        )

    def remote(source, target, device):
        copy = describe(source, target, device)
        copy.start()
        sends.append(copy)
        return copy

    fld[0] = jnp.zeros((128, 128), F32)
    fld[9] = jnp.zeros((128, 128), F32)
    for copy in field_loads:
        copy.wait()
    for y in range(8):
        halo_s[0, y] = fld[y + 1, pl.ds(0, 16, stride=8), :]
        halo_s[1, y] = fld[y + 1, pl.ds(7, 16, stride=8), :]
    keep = jnp.where(gz == lax.axis_size("gz") - 1, 0.0, 1.0).astype(F32)
    for copy in cond_loads:
        copy.wait()

    def plane(buf, y, f, z):
        return buf[y, pl.ds(pl.multiple_of(f * 32 + z * 8, 8), 8), :]

    def eliminate_mass(owner, p):
        f, y = owner * 2 + p // 8, lax.rem(p, 8)
        e = owner * 16 + p
        block = (plane(cnd, y, f, 0), 1.0, 0.0)
        for z in (1, 2, 3):
            face = plane(cnd, y, f, z)
            if z == 3:
                face = face * keep
            block, held = merge_mass(block, (face, 1.0, 0.0))
            for n in range(3):
                coef[e, 3 * z - 3 + n] = held[n]
        return block

    @pl.loop(0, 16, unroll=4)
    def _(p):
        block = eliminate_mass(other, p)
        for n in range(3):
            pair_cs[p, n] = block[n]

    edges = lax.min(xy, 1) + lax.min(n_xy - 1 - xy, 1)
    pl.semaphore_wait(barrier, len(partners) + edges)
    to_left = describe(halo_s.at[0], halo_r.at[1], left)
    to_right = describe(halo_s.at[1], halo_r.at[0], right)
    sides = ((has_left, to_left, to_right, 0), (has_right, to_right, to_left, 1))
    for present, outward, unused, unused_side in sides:
        @pl.when(present)
        def _(outward=outward):
            outward.start()

    pair_c = remote(pair_cs, blk_c.at[core], peer)

    @pl.loop(0, 16, unroll=4)
    def _(p):
        block = eliminate_mass(core, p)
        for n in range(3):
            blk_c[core, p, n] = block[n]

    def powers(j):
        power = arm[j]
        wsc[j] = jnp.full((32, ARM), 1.0 / ARM, F32)
        last = lax.broadcasted_iota(jnp.int32, (ARM, SUB), 0) == ARM - 1
        gsc[j] = jnp.where(last, 1.0, 0.0).astype(F32)
        n = 1
        while n < SUB:
            both = dot(jnp.concatenate([power, wsc[j, 0:8]], axis=0), power, HIGH)
            tips = dot(power, gsc[j], HIGH)
            wsc[j, n : 2 * n] = both[ARM : ARM + n]
            gsc[j, :, n : 2 * n] = tips[:, 0:n]
            power = both[:ARM]
            n *= 2
        wsc[j, SUB : SUB + 1] = jnp.sum(power, axis=0, keepdims=True) * (1.0 / ARM)
        rows = wsc[j]
        end = lax.broadcasted_iota(jnp.int32, (SUB, ARM), 1) == ARM - 1
        held = jnp.sum(jnp.where(end, rows[:SUB], 0.0), axis=1, keepdims=True)
        hsc[j] = jnp.broadcast_to(held, (SUB, 128))
        for n, part in enumerate(split(rows)):
            lhs1[j, :, 128 * n : 128 * n + 64] = part
            lhs1[j, :, 128 * n + 64 : 128 * n + 128] = part
        high, low = split(power)
        lhs2[j, :, 0:64] = high
        lhs2[j, :, 64:128] = high
        lhs2[j, :, 128:192] = low
        high, low = split(gsc[j])
        lhs2[j, :, 192:208] = high
        lhs2[j, :, 208:224] = high
        lhs2[j, :, 224:240] = low
        lhs2[j, :, 240:256] = low

    def part_at(i):
        return lax.rem(chip + (CHIPS - i), CHIPS)

    pair_c.wait_recv()
    for i in range(CHIPS):
        p = part_at(i)
        merged, held = merge_mass(*([blk_c[c, p, n] for n in range(3)] for c in range(2)))
        target = ring_cs if TO[i] else ring_cr
        for n in range(3):
            chip_coef[i, n] = held[n]
            target[i, n] = merged[n]
    ring_c = [remote(ring_cs.at[i], ring_cr.at[i], at_chip(TO[i])) for i in SENT]

    for copy in small_loads:
        copy.wait()
    row = lax.broadcasted_iota(jnp.int32, (8, 128), 0)
    lane = lax.broadcasted_iota(jnp.int32, (8, 128), 1)

    @pl.loop(0, 16)
    def _(q):
        at = pl.ds(pl.multiple_of(q * 8, 8), 8)
        rate = lateral[q // 4]
        tiles = [fld[y, at, :] for y in range(10)]
        for y in range(8):
            before, here, after = tiles[y : y + 3]
            down = jnp.where(row == 0, 0.0, pltpu.roll(here, 1, 0))
            up = jnp.where(row == 7, 0.0, pltpu.roll(here, 7, 0))
            low = pltpu.roll(jnp.where(lane == 127, before, here), 1, 1)
            high = pltpu.roll(jnp.where(lane == 0, after, here), 127, 1)
            src[y, at, :] = here + rate * (down + up + low + high - 4.0 * here)

    for present, unused, inward, side in sides:
        @pl.when(present)
        def _(inward=inward):
            inward.wait_recv()

        @pl.when(jnp.logical_not(present))
        def _(side=side):
            halo_r[side] = jnp.zeros((8, 16, 128), F32)

    def eliminate_rhs(owner, p):
        f, y = owner * 2 + p // 8, lax.rem(p, 8)
        e = owner * 16 + p
        rate = lateral[f]
        block = None
        for z in range(4):
            edge = jnp.where(row == 0, halo_r[0, y, pl.ds(f * 4 + z, 1), :] * rate, 0.0)
            edge += jnp.where(row == 7, halo_r[1, y, pl.ds(f * 4 + z, 1), :] * rate, 0.0)
            here = plane(src, y, f, z) + edge
            if z == 0:
                block = (here, 0.0)
            else:
                block, tail[e, z - 1] = merge_rhs(
                    block, (here, 0.0), *(coef[e, 3 * z - 3 + n] for n in range(3))
                )
        return block

    @pl.loop(0, 16, unroll=4)
    def _(p):
        block = eliminate_rhs(other, p)
        for n in range(2):
            pair_rs[p, n] = block[n]

    pair_r = remote(pair_rs, blk_r.at[core], peer)

    @pl.loop(0, 16, unroll=4)
    def _(p):
        block = eliminate_rhs(core, p)
        for n in range(2):
            blk_r[core, p, n] = block[n]

    pair_r.wait_recv()
    for i in range(CHIPS):
        p = part_at(i)
        merged, chip_coef[i, 2] = merge_rhs(
            *([blk_r[c, p, n] for n in range(2)] for c in range(2)),
            *(chip_coef[i, n] for n in range(3)),
        )
        target = ring_rs if TO[i] else ring_rr
        for n in range(2):
            target[i, n] = merged[n]
    ring_r = [remote(ring_rs.at[i], ring_rr.at[i], at_chip(TO[i])) for i in SENT]

    for j in range(3):
        powers(j)


    for copy in ring_c:
        copy.wait_recv()
    for half in range(2):
        masses = [[ring_cr[half * HALF + b, n] for n in range(3)] for b in range(HALF)]
        at = 0
        while len(masses) > 1:
            joined = [merge_mass(*masses[b : b + 2]) for b in range(0, len(masses), 2)]
            masses = [block for block, held in joined]
            for block, held in joined:
                for n in range(3):
                    top_coef[half, at, n] = held[n]
                at += 1
        for n in range(3):
            half_cs[half, n] = masses[0][n]
    across = (at_chip(REACH), at_chip(-REACH))
    half_c = [remote(half_cs.at[h], half_cr.at[1 - h], across[h]) for h in range(2)]

    for copy in prof_loads:
        copy.wait()

    def tile_pair(j, t):
        at = [pl.multiple_of(j * 1024 + t * 128 + 64 * n, 64) for n in range(2)]
        return at, jnp.concatenate([prof[pl.ds(a, 64), :] for a in at], axis=1)

    @pl.loop(0, 8)
    def _(t):
        for j in range(3):
            unused, tile = tile_pair(j, t)
            high, low = (part.astype(BF16) for part in split(tile))
            means = dot(lhs1[j].astype(BF16), jnp.concatenate([high, low, high, low], axis=0))
            for n in range(2):
                ysc[j, pl.ds(pl.multiple_of(t * 64 + 32 * n, 32), 32), :] = means[:, 128 * n : 128 * n + 128]

    for slot in range(SLOTS):
        tile = ids[0, slot]
        y, at = lax.rem(tile, 8), (tile // 64) * 8 + lax.rem(tile // 8, 8)
        for f in range(4):
            cells[f, slot : slot + 1] = fld[y + 1, pl.ds(f * 32 + at, 1), :]

    live = lax.broadcasted_iota(jnp.int32, (SLOTS, 128), 0) < count[0]
    solid = 0.9 / (1.0 + jnp.exp(cells[3]))
    inverses = [1.0 / (1.0 - solid * ((k + 1) / SUB)) for k in range(SUB)]
    for j in range(3):
        solute = cells[j]
        half = 0.5 * partition[j]
        liquids = []
        for k in range(SUB + 1):
            mean = ysc[j, pl.ds(k, SLOTS, stride=32), :]
            for i in range(k):
                mean += hsc[j, k - 1 - i : k - i, :] * liquids[i]
            if k == SUB:
                moved = solid * (mean - partition[j] * solute)
                change[:, 128 * j : 128 * j + 128] = jnp.where(live, moved, 0.0)
            else:
                fraction = solid * ((k + 1) / SUB)
                liquids.append(half * ((solute - fraction * mean) * inverses[k]))
                ssc[j, pl.ds(SUB - 1 - k, SLOTS, stride=SUB), :] = liquids[k]

    for copy in ring_r:
        copy.wait_recv()
    levels = ([], [])
    for half in range(2):
        rhs = [[ring_rr[half * HALF + b, n] for n in range(2)] for b in range(HALF)]
        at = 0
        while len(rhs) > 1:
            level, joined = [], []
            for b in range(0, len(rhs), 2):
                block, top_coef[half, at, 2] = merge_rhs(
                    rhs[b], rhs[b + 1], *(top_coef[half, at, n] for n in range(3))
                )
                joined.append(block)
                level.append(at)
                at += 1
            rhs = joined
            levels[half].append(level)
        for n in range(2):
            half_rs[half, n] = rhs[0][n]
    half_r = [remote(half_rs.at[h], half_rr.at[1 - h], across[h]) for h in range(2)]

    def evolve(j):
        @pl.loop(0, 8)
        def _(t):
            at, tile = tile_pair(j, t)
            tips = jnp.concatenate(
                [ssc[j, pl.ds(pl.multiple_of(t * 32 + 16 * n, 16), 16), :] for n in range(2)], axis=1
            )
            high, low = (part.astype(BF16) for part in split(tile))
            tip_high, tip_low = (part.astype(BF16) for part in split(tips))
            evolved = dot(
                lhs2[j].astype(BF16),
                jnp.concatenate(
                    [high, low, high, tip_high, tip_low, tip_high, tip_low], axis=0
                ),
            )
            for n in range(2):
                shown = jnp.full((ARM, 128), 2 * t + n, jnp.int32) < count[0]
                out_profiles[pl.ds(at[n], 64), :] = jnp.where(
                    shown, evolved[:, 128 * n : 128 * n + 128], 0.0
                )

    evolve(0)

    for copy in half_c + half_r:
        copy.wait_recv()
    for half in range(2):
        own, met = (half_cs, half_rs), (half_cr, half_rr)
        lower, upper = (own, met) if half == 0 else (met, own)
        whole, held = merge_mass(*([buf[0][half, n] for n in range(3)] for buf in (lower, upper)))
        total, ratio = merge_rhs(
            *([buf[1][half, n] for n in range(2)] for buf in (lower, upper)), *held
        )
        start = (total[0] + total[1]) / (whole[1] + whole[2])
        middle = ratio + (held[0] + held[1]) * start
        values = [start, middle] if half == 0 else [middle, start]
        for level in reversed(levels[half]):
            finer = [values[0]]
            for b, at in enumerate(level):
                a, c, ratio = (top_coef[half, at, n] for n in range(3))
                finer += [ratio + a * values[b] + c * values[b + 1], values[b + 1]]
            values = finer
        for b in range(HALF):
            i = half * HALF + b
            target = ret_s if TO[i] else ret_r
            for n in range(2):
                target[i, n] = values[b + n]
    ret = [remote(ret_s.at[i], ret_r.at[i], at_chip(-TO[i])) for i in SENT]

    evolve(1)
    evolve(2)

    place = lax.broadcasted_iota(jnp.int32, (256, SLOTS), 0)
    named = (place // 64) * 64 + lax.rem(place, 8) * 8 + lax.rem(place // 8, 8)
    hit = jnp.where(named == ids_row[...], 1.0, 0.0).astype(BF16)
    rest = change[...]
    spreads = None
    for n in range(3):
        piece = rest.astype(BF16)
        rest = rest - piece.astype(F32)
        term = dot(hit, piece)
        spreads = term if spreads is None else spreads + term
    for j in range(3):
        delta[j] = spreads[:, 128 * j : 128 * j + 128]
    delta[3] = jnp.zeros((256, 128), F32)

    for copy in ret:
        copy.wait_recv()
    for i in range(CHIPS):
        p = part_at(i)
        low, high = ret_r[i, 0], ret_r[i, 1]
        middle = chip_coef[i, 2] + chip_coef[i, 0] * low + chip_coef[i, 1] * high
        fin[0, p, 0] = low
        fin[0, p, 1] = middle
        fin[1, p, 0] = middle
        fin[1, p, 1] = high
    last = remote(fin.at[other], fin_r, peer)

    def finish(owner, p, low, high):
        f, y = owner * 2 + p // 8, lax.rem(p, 8)
        e = owner * 16 + p
        above = high
        values = [low, None, None, None]
        for z in (3, 2, 1):
            above = tail[e, z - 1] + coef[e, 3 * z - 3] * low + coef[e, 3 * z - 2] * above
            values[z] = above
        lanes = pl.ds(pl.multiple_of(y * 128, 128), 128)
        for z in range(4):
            at = pl.ds(pl.multiple_of(f * 32 + z * 8, 8), 8)
            out_fields[at, lanes] = values[z] + delta[f, pl.ds(pl.multiple_of(z * 64 + y * 8, 8), 8), :]

    @pl.loop(0, 16, unroll=4)
    def _(p):
        finish(core, p, fin[core, p, 0], fin[core, p, 1])

    last.wait_recv()

    @pl.loop(0, 16, unroll=4)
    def _(p):
        finish(other, p, fin_r[p, 0], fin_r[p, 1])

    for present, outward, unused, unused_side in sides:
        @pl.when(present)
        def _(outward=outward):
            outward.wait_send()

    for copy in sends:
        copy.wait_send()


def deliver(new_fields, new_profiles, out_fields, out_profiles, sem):
    copies = []
    for ref, out, rows, pieces in (
        (new_profiles, out_profiles, 512, 6), (new_fields, out_fields, 64, 2),
    ):
        for n in range(pieces):
            part = pl.ds(rows * n, rows)
            copies.append(pltpu.make_async_copy(ref.at[part], out.at[part], sem.at[len(copies)]))
    for copy in copies:
        copy.start()
    for copy in copies:
        copy.wait()


def body(fields, conductance, lateral, partition, arm_step, profiles, tile_ids, tile_count):
    tile = (8, 128)
    scratch = [
        (10, 128, 128), (8, 128, 128), (8, 128, 128), (3072, 128), (32, 9) + tile, (32, 3) + tile,
        (2, 8, 16, 128), (2, 8, 16, 128),
        (16, 3) + tile, (16, 2) + tile, (2, 16, 3) + tile, (2, 16, 2) + tile, (16, 3) + tile,
        (16, 3) + tile, (16, 2) + tile, (16, 3) + tile, (16, 2) + tile,
        (2, 3) + tile, (2, 2) + tile, (2, 3) + tile, (2, 2) + tile,
        (16, 2) + tile, (16, 2) + tile, (2, 16, 2) + tile, (16, 2) + tile, (2, 7, 3) + tile,
        (4, 16, 128), (3, 32, 64), (3, 64, 16), (3, 16, 128), (3, 32, 256), (3, 64, 256),
        (3, 512, 128), (3, 256, 128), (16, 384), (4, 256, 128),
    ]
    hbm = pl.BlockSpec(memory_space=pl.ANY)
    vmem = pl.BlockSpec(memory_space=pltpu.VMEM)
    operands = [
        pltpu.with_memory_space_constraint(x, pltpu.HBM)
        for x in (
            fields.reshape(128, 1024), conductance.reshape(128, 1024), lateral, partition,
            arm_step, profiles.reshape(3072, 128), tile_ids,
        )
    ]
    new_fields, new_profiles = pl.pallas_call(
        functools.partial(kernel, lax.axis_size("xy")),
        out_shape=(pltpu.VMEM((128, 1024), F32), pltpu.VMEM((3072, 128), F32)),
        in_specs=[hbm] * 7 + [pl.BlockSpec(memory_space=pltpu.SMEM)],
        out_specs=(vmem, vmem),
        scratch_shapes=[
            pltpu.SMEM((4,), F32), pltpu.SMEM((3,), F32),
            pltpu.SMEM((1, SLOTS), jnp.int32),
            pltpu.VMEM((1, SLOTS), jnp.int32), pltpu.VMEM((3, ARM, ARM), F32),
        ]
        + [pltpu.VMEM(shape, F32) for shape in scratch]
        + [
            pltpu.SemaphoreType.DMA((16,)),
            pltpu.SemaphoreType.DMA((5,)),
            pltpu.SemaphoreType.DMA((3,)),
            pltpu.SemaphoreType.DMA((51,)),
            pltpu.SemaphoreType.DMA((51,)),
        ],
        compiler_params=pltpu.CompilerParams(
            collective_id=0, has_side_effects=True, vmem_limit_bytes=40 * 2**20
        ),
        cost_estimate=pl.CostEstimate(flops=10**9, bytes_accessed=5 * 2**20, transcendentals=2048),
        name="ingot",
    )(*operands, tile_count)
    new_fields, new_profiles = pl.pallas_call(
        deliver,
        out_shape=(pltpu.HBM((128, 1024), F32), pltpu.HBM((3072, 128), F32)),
        in_specs=[vmem, vmem],
        out_specs=(hbm, hbm),
        scratch_shapes=[pltpu.SemaphoreType.DMA((8,))],
        cost_estimate=pl.CostEstimate(flops=0, bytes_accessed=2**22, transcendentals=0),
        name="deliver",
    )(
        pltpu.with_memory_space_constraint(new_fields, pltpu.VMEM),
        pltpu.with_memory_space_constraint(new_profiles, pltpu.VMEM),
    )
    return new_fields.reshape(fields.shape), new_profiles.reshape(profiles.shape)


def solution(mesh):
    return jax.shard_map(
        body,
        mesh=mesh,
        in_specs=(
            P(None, "gz", "xy", None),
            P(None, "gz", "xy", None),
            P(),
            P(),
            P(),
            P(None, ("gz", "xy"), None, None),
            P(("gz", "xy"), None),
            P(("gz", "xy")),
        ),
        out_specs=(P(None, "gz", "xy", None), P(None, ("gz", "xy"), None, None)),
        check_vma=False,
    )
```

```python
import functools

import jax
import jax.numpy as jnp
from jax import lax
from jax.experimental import pallas as pl
from jax.experimental.pallas import tpu as pltpu
from jax.sharding import PartitionSpec as P

F32 = jnp.float32
BF16 = jnp.bfloat16
MESH = pl.DeviceIdType.MESH
HIGH = lax.Precision.HIGHEST
SUB = 16
ARM = 64
SLOTS = 16
CHIPS = 16
HALF = CHIPS // 2
REACH = 5
KNOWN = 3
TO = [REACH - i for i in range(HALF)] + [2 * REACH - i for i in range(HALF, CHIPS)]
PLACES = sorted(range(CHIPS), key=lambda i: (-abs(TO[i]), i))
SENT = PLACES[:-2]
OUT = ((0, 4), (4, 8), (8, 12), (12, 16))
BACK = ((10, 16), (4, 10), (0, 4))


def merge_mass(low, high):
    mass = low[2] + high[1]
    inverse = 1.0 / (mass + low[0] + high[0])
    a, b = low[0] * inverse, high[0] * inverse
    return (a * high[0], low[1] + a * mass, high[2] + b * mass), (a, b, inverse)


def merge_rhs(low, high, a, b, inverse):
    rhs = low[1] + high[0]
    return (low[0] + a * rhs, high[1] + b * rhs), rhs * inverse


def split(x):
    high = x.astype(BF16).astype(F32)
    return high, x - high


def dot(x, y, precision=None):
    return jnp.dot(x, y, precision=precision, preferred_element_type=F32)


def kernel(
    n_xy,
    fields, cond, lateral_in, partition_in, arm_in, profiles, ids_in, count,
    out_fields, out_profiles,
    lateral, partition, ids, ids_row, arm,
    fld, cnd, src, prof, coef, tail,
    halo_s, halo_r,
    pair_cs, pair_rs, blk_c, blk_r, chip_coef,
    ring_cs, ring_rs, ring_cr, ring_rr, half_cs, half_rs, half_cr, half_rr,
    ret_s, ret_r, fin, fin_r, top_coef,
    cells, wsc, gsc, hsc, lhs1, lhs2, ysc, ssc, change, delta,
    in_sem, small_sem, prof_sem,
    send_sem, recv_sem, near_sem,
):
    gz = lax.axis_index("gz")
    xy = lax.axis_index("xy")
    core = lax.rem(gz, 2)
    chip = gz // 2
    other = 1 - core

    def at_chip(offset):
        return (lax.rem(chip + (offset + CHIPS), CHIPS) * 2 + core, xy)

    left = (gz, lax.rem(xy + n_xy - 1, n_xy))
    right = (gz, lax.rem(xy + 1, n_xy))
    peer = (chip * 2 + other, xy)

    def load(ref, buf, base, y, sem):
        return pltpu.make_async_copy(
            ref.at[:, pl.ds(128 * y, 128)], buf.at[y + base], in_sem.at[sem + y]
        )

    field_loads = [load(fields, fld, 1, y, 0) for y in range(8)]
    cond_loads = [load(cond, cnd, 0, y, 8) for y in range(8)]
    prof_loads = [
        pltpu.make_async_copy(
            profiles.at[pl.ds(1024 * j, 1024)], prof.at[pl.ds(1024 * j, 1024)], prof_sem.at[j]
        )
        for j in range(3)
    ]
    small = [(lateral_in, lateral), (partition_in, partition), (ids_in, ids)]
    small += [(ids_in, ids_row), (arm_in, arm)]
    small_loads = [
        pltpu.make_async_copy(ref, buf, small_sem.at[n]) for n, (ref, buf) in enumerate(small)
    ]
    barrier = pltpu.get_barrier_semaphore()
    has_left, has_right = xy > 0, xy < n_xy - 1

    partners = [at_chip(d * sign) for d in range(KNOWN, 0, -1) for sign in (1, -1)] + [peer]
    for partner in partners:
        pl.semaphore_signal(barrier, inc=1, device_id=partner, device_id_type=MESH)
    @pl.when(has_left)
    def _():
        pl.semaphore_signal(barrier, inc=1, device_id=left, device_id_type=MESH)

    @pl.when(has_right)
    def _():
        pl.semaphore_signal(barrier, inc=1, device_id=right, device_id_type=MESH)

    for copy in field_loads + cond_loads + small_loads:
        copy.start()

    sends = []
    used = [0]

    def describe(source, target, device):
        n = used[0]
        used[0] = n + 1
        return pltpu.make_async_remote_copy(
            src_ref=source, dst_ref=target, send_sem=send_sem.at[n], recv_sem=recv_sem.at[n],
            device_id=device, device_id_type=MESH,
        )

    def remote(source, target, device):
        copy = describe(source, target, device)
        copy.start()
        sends.append(copy)
        return copy

    fld[0] = jnp.zeros((128, 128), F32)
    fld[9] = jnp.zeros((128, 128), F32)
    for copy in field_loads:
        copy.wait()
    for y in range(8):
        halo_s[0, y] = fld[y + 1, pl.ds(0, 16, stride=8), :]
        halo_s[1, y] = fld[y + 1, pl.ds(7, 16, stride=8), :]
    keep = jnp.where(gz == lax.axis_size("gz") - 1, 0.0, 1.0).astype(F32)
    for copy in cond_loads:
        copy.wait()

    def plane(buf, y, f, z):
        return buf[y, pl.ds(pl.multiple_of(f * 32 + z * 8, 8), 8), :]

    def eliminate_mass(owner, p):
        f, y = owner * 2 + p // 8, lax.rem(p, 8)
        e = owner * 16 + p
        block = (plane(cnd, y, f, 0), 1.0, 0.0)
        for z in (1, 2, 3):
            face = plane(cnd, y, f, z)
            if z == 3:
                face = face * keep
            block, held = merge_mass(block, (face, 1.0, 0.0))
            for n in range(3):
                coef[e, 3 * z - 3 + n] = held[n]
        return block

    @pl.loop(0, 16, unroll=4)
    def _(p):
        block = eliminate_mass(other, p)
        for n in range(3):
            pair_cs[p, n] = block[n]

    edges = lax.min(xy, 1) + lax.min(n_xy - 1 - xy, 1)
    pl.semaphore_wait(barrier, len(partners) + edges)
    for sign in (1, -1):
        pl.semaphore_signal(
            near_sem, inc=1, device_id=at_chip(sign * (REACH - KNOWN)), device_id_type=MESH
        )
    to_left = describe(halo_s.at[0], halo_r.at[1], left)
    to_right = describe(halo_s.at[1], halo_r.at[0], right)
    sides = ((has_left, to_left, to_right, 0), (has_right, to_right, to_left, 1))
    for present, outward, unused, unused_side in sides:
        @pl.when(present)
        def _(outward=outward):
            outward.start()

    for copy in prof_loads:
        copy.start()
    pair_c = remote(pair_cs, blk_c.at[core], peer)

    @pl.loop(0, 16, unroll=4)
    def _(p):
        block = eliminate_mass(core, p)
        for n in range(3):
            blk_c[core, p, n] = block[n]

    def powers(j):
        power = arm[j]
        wsc[j] = jnp.full((32, ARM), 1.0 / ARM, F32)
        last = lax.broadcasted_iota(jnp.int32, (ARM, SUB), 0) == ARM - 1
        gsc[j] = jnp.where(last, 1.0, 0.0).astype(F32)
        n = 1
        while n < SUB:
            both = dot(jnp.concatenate([power, wsc[j, 0:8]], axis=0), power, HIGH)
            tips = dot(power, gsc[j], HIGH)
            wsc[j, n : 2 * n] = both[ARM : ARM + n]
            gsc[j, :, n : 2 * n] = tips[:, 0:n]
            power = both[:ARM]
            n *= 2
        wsc[j, SUB : SUB + 1] = jnp.sum(power, axis=0, keepdims=True) * (1.0 / ARM)
        rows = wsc[j]
        end = lax.broadcasted_iota(jnp.int32, (SUB, ARM), 1) == ARM - 1
        held = jnp.sum(jnp.where(end, rows[:SUB], 0.0), axis=1, keepdims=True)
        hsc[j] = jnp.broadcast_to(held, (SUB, 128))
        for n, part in enumerate(split(rows)):
            lhs1[j, :, 128 * n : 128 * n + 64] = part
            lhs1[j, :, 128 * n + 64 : 128 * n + 128] = part
        high, low = split(power)
        lhs2[j, :, 0:64] = high
        lhs2[j, :, 64:128] = high
        lhs2[j, :, 128:192] = low
        high, low = split(gsc[j])
        lhs2[j, :, 192:208] = high
        lhs2[j, :, 208:224] = high
        lhs2[j, :, 224:240] = low
        lhs2[j, :, 240:256] = low

    def part_at(i):
        return lax.rem(chip + (CHIPS - i), CHIPS)

    pair_c.wait_recv()
    for i in range(CHIPS):
        p = part_at(i)
        merged, held = merge_mass(*([blk_c[c, p, n] for n in range(3)] for c in range(2)))
        target = ring_cs if TO[i] else ring_cr
        for n in range(3):
            chip_coef[i, n] = held[n]
            target[i, n] = merged[n]
    def send_mass(far):
        return [
            remote(ring_cs.at[i], ring_cr.at[i], at_chip(TO[i]))
            for i in SENT
            if (abs(TO[i]) > KNOWN) == far
        ]

    ring_c = send_mass(False)
    pl.semaphore_wait(near_sem, 2)
    ring_c += send_mass(True)


    for copy in small_loads:
        copy.wait()
    row = lax.broadcasted_iota(jnp.int32, (8, 128), 0)
    lane = lax.broadcasted_iota(jnp.int32, (8, 128), 1)

    @pl.loop(0, 16)
    def _(q):
        at = pl.ds(pl.multiple_of(q * 8, 8), 8)
        rate = lateral[q // 4]
        tiles = [fld[y, at, :] for y in range(10)]
        for y in range(8):
            before, here, after = tiles[y : y + 3]
            down = jnp.where(row == 0, 0.0, pltpu.roll(here, 1, 0))
            up = jnp.where(row == 7, 0.0, pltpu.roll(here, 7, 0))
            low = pltpu.roll(jnp.where(lane == 127, before, here), 1, 1)
            high = pltpu.roll(jnp.where(lane == 0, after, here), 127, 1)
            src[y, at, :] = here + rate * (down + up + low + high - 4.0 * here)

    for present, unused, inward, side in sides:
        @pl.when(present)
        def _(inward=inward):
            inward.wait_recv()

        @pl.when(jnp.logical_not(present))
        def _(side=side):
            halo_r[side] = jnp.zeros((8, 16, 128), F32)

    def eliminate_rhs(owner, p):
        f, y = owner * 2 + p // 8, lax.rem(p, 8)
        e = owner * 16 + p
        rate = lateral[f]
        block = None
        for z in range(4):
            edge = jnp.where(row == 0, halo_r[0, y, pl.ds(f * 4 + z, 1), :] * rate, 0.0)
            edge += jnp.where(row == 7, halo_r[1, y, pl.ds(f * 4 + z, 1), :] * rate, 0.0)
            here = plane(src, y, f, z) + edge
            if z == 0:
                block = (here, 0.0)
            else:
                block, tail[e, z - 1] = merge_rhs(
                    block, (here, 0.0), *(coef[e, 3 * z - 3 + n] for n in range(3))
                )
        return block

    pair_r = []
    for begin, end in OUT:
        for k in range(begin, end):
            block = eliminate_rhs(other, part_at(PLACES[k]))
            for n in range(2):
                pair_rs[k, n] = block[n]
        piece = pl.ds(begin, end - begin)
        pair_r.append(remote(pair_rs.at[piece], blk_r.at[core, piece], peer))
    for k in range(CHIPS):
        block = eliminate_rhs(core, part_at(PLACES[k]))
        for n in range(2):
            blk_r[core, k, n] = block[n]

    ring_r = []
    for copy, (begin, end) in zip(pair_r, OUT):
        copy.wait_recv()
        for k in range(begin, end):
            i = PLACES[k]
            merged, chip_coef[i, 2] = merge_rhs(
                *([blk_r[c, k, n] for n in range(2)] for c in range(2)),
                *(chip_coef[i, n] for n in range(3)),
            )
            target = ring_rs if TO[i] else ring_rr
            for n in range(2):
                target[i, n] = merged[n]
        for i in PLACES[begin:end]:
            if TO[i]:
                ring_r.append(remote(ring_rs.at[i], ring_rr.at[i], at_chip(TO[i])))

    for j in range(3):
        powers(j)


    for copy in ring_c:
        copy.wait_recv()
    for half in range(2):
        masses = [[ring_cr[half * HALF + b, n] for n in range(3)] for b in range(HALF)]
        at = 0
        while len(masses) > 1:
            joined = [merge_mass(*masses[b : b + 2]) for b in range(0, len(masses), 2)]
            masses = [block for block, held in joined]
            for block, held in joined:
                for n in range(3):
                    top_coef[half, at, n] = held[n]
                at += 1
        for n in range(3):
            half_cs[half, n] = masses[0][n]
    across = (at_chip(REACH), at_chip(-REACH))
    half_c = [remote(half_cs.at[h], half_cr.at[1 - h], across[h]) for h in range(2)]

    for copy in prof_loads:
        copy.wait()

    def tile_pair(j, t):
        at = [pl.multiple_of(j * 1024 + t * 128 + 64 * n, 64) for n in range(2)]
        return at, jnp.concatenate([prof[pl.ds(a, 64), :] for a in at], axis=1)

    @pl.loop(0, 8)
    def _(t):
        for j in range(3):
            unused, tile = tile_pair(j, t)
            high, low = (part.astype(BF16) for part in split(tile))
            means = dot(lhs1[j].astype(BF16), jnp.concatenate([high, low, high, low], axis=0))
            for n in range(2):
                ysc[j, pl.ds(pl.multiple_of(t * 64 + 32 * n, 32), 32), :] = means[:, 128 * n : 128 * n + 128]

    for slot in range(SLOTS):
        tile = ids[0, slot]
        y, at = lax.rem(tile, 8), (tile // 64) * 8 + lax.rem(tile // 8, 8)
        for f in range(4):
            cells[f, slot : slot + 1] = fld[y + 1, pl.ds(f * 32 + at, 1), :]

    live = lax.broadcasted_iota(jnp.int32, (SLOTS, 128), 0) < count[0]
    solid = 0.9 / (1.0 + jnp.exp(cells[3]))
    inverses = [1.0 / (1.0 - solid * ((k + 1) / SUB)) for k in range(SUB)]
    for j in range(3):
        solute = cells[j]
        half = 0.5 * partition[j]
        liquids = []
        for k in range(SUB + 1):
            mean = ysc[j, pl.ds(k, SLOTS, stride=32), :]
            for i in range(k):
                mean += hsc[j, k - 1 - i : k - i, :] * liquids[i]
            if k == SUB:
                moved = solid * (mean - partition[j] * solute)
                change[:, 128 * j : 128 * j + 128] = jnp.where(live, moved, 0.0)
            else:
                fraction = solid * ((k + 1) / SUB)
                liquids.append(half * ((solute - fraction * mean) * inverses[k]))
                ssc[j, pl.ds(SUB - 1 - k, SLOTS, stride=SUB), :] = liquids[k]

    for copy in ring_r:
        copy.wait_recv()
    levels = ([], [])
    for half in range(2):
        rhs = [[ring_rr[half * HALF + b, n] for n in range(2)] for b in range(HALF)]
        at = 0
        while len(rhs) > 1:
            level, joined = [], []
            for b in range(0, len(rhs), 2):
                block, top_coef[half, at, 2] = merge_rhs(
                    rhs[b], rhs[b + 1], *(top_coef[half, at, n] for n in range(3))
                )
                joined.append(block)
                level.append(at)
                at += 1
            rhs = joined
            levels[half].append(level)
        for n in range(2):
            half_rs[half, n] = rhs[0][n]
    half_r = [remote(half_rs.at[h], half_rr.at[1 - h], across[h]) for h in range(2)]

    def evolve(j):
        @pl.loop(0, 8)
        def _(t):
            at, tile = tile_pair(j, t)
            tips = jnp.concatenate(
                [ssc[j, pl.ds(pl.multiple_of(t * 32 + 16 * n, 16), 16), :] for n in range(2)], axis=1
            )
            high, low = (part.astype(BF16) for part in split(tile))
            tip_high, tip_low = (part.astype(BF16) for part in split(tips))
            evolved = dot(
                lhs2[j].astype(BF16),
                jnp.concatenate(
                    [high, low, high, tip_high, tip_low, tip_high, tip_low], axis=0
                ),
            )
            for n in range(2):
                shown = jnp.full((ARM, 128), 2 * t + n, jnp.int32) < count[0]
                out_profiles[pl.ds(at[n], 64), :] = jnp.where(
                    shown, evolved[:, 128 * n : 128 * n + 128], 0.0
                )

    evolve(0)

    for copy in half_c + half_r:
        copy.wait_recv()
    for half in range(2):
        own, met = (half_cs, half_rs), (half_cr, half_rr)
        lower, upper = (own, met) if half == 0 else (met, own)
        whole, held = merge_mass(*([buf[0][half, n] for n in range(3)] for buf in (lower, upper)))
        total, ratio = merge_rhs(
            *([buf[1][half, n] for n in range(2)] for buf in (lower, upper)), *held
        )
        start = (total[0] + total[1]) / (whole[1] + whole[2])
        middle = ratio + (held[0] + held[1]) * start
        values = [start, middle] if half == 0 else [middle, start]
        for level in reversed(levels[half]):
            finer = [values[0]]
            for b, at in enumerate(level):
                a, c, ratio = (top_coef[half, at, n] for n in range(3))
                finer += [ratio + a * values[b] + c * values[b + 1], values[b + 1]]
            values = finer
        for b in range(HALF):
            i = half * HALF + b
            target = ret_s if TO[i] else ret_r
            for n in range(2):
                target[i, n] = values[b + n]
    ret = {i: remote(ret_s.at[i], ret_r.at[i], at_chip(-TO[i])) for i in SENT}

    evolve(1)
    evolve(2)

    place = lax.broadcasted_iota(jnp.int32, (256, SLOTS), 0)
    named = (place // 64) * 64 + lax.rem(place, 8) * 8 + lax.rem(place // 8, 8)
    hit = jnp.where(named == ids_row[...], 1.0, 0.0).astype(BF16)
    rest = change[...]
    spreads = None
    for n in range(3):
        piece = rest.astype(BF16)
        rest = rest - piece.astype(F32)
        term = dot(hit, piece)
        spreads = term if spreads is None else spreads + term
    for j in range(3):
        delta[j] = spreads[:, 128 * j : 128 * j + 128]
    delta[3] = jnp.zeros((256, 128), F32)

    def finish(owner, p, low, high):
        f, y = owner * 2 + p // 8, lax.rem(p, 8)
        e = owner * 16 + p
        above = high
        values = [low, None, None, None]
        for z in (3, 2, 1):
            above = tail[e, z - 1] + coef[e, 3 * z - 3] * low + coef[e, 3 * z - 2] * above
            values[z] = above
        lanes = pl.ds(pl.multiple_of(y * 128, 128), 128)
        for z in range(4):
            at = pl.ds(pl.multiple_of(f * 32 + z * 8, 8), 8)
            out_fields[at, lanes] = values[z] + delta[f, pl.ds(pl.multiple_of(z * 64 + y * 8, 8), 8), :]

    last = []
    for begin, end in BACK:
        for i in PLACES[begin:end]:
            if TO[i]:
                ret[i].wait_recv()
        for k in range(begin, end):
            i = PLACES[k]
            low, high = ret_r[i, 0], ret_r[i, 1]
            middle = chip_coef[i, 2] + chip_coef[i, 0] * low + chip_coef[i, 1] * high
            fin[0, k, 0] = low
            fin[0, k, 1] = middle
            fin[1, k, 0] = middle
            fin[1, k, 1] = high
        piece = pl.ds(begin, end - begin)
        last.append(remote(fin.at[other, piece], fin_r.at[piece], peer))
        for k in range(begin, end):
            finish(core, part_at(PLACES[k]), fin[core, k, 0], fin[core, k, 1])
    for copy, (begin, end) in zip(last, BACK):
        copy.wait_recv()
        for k in range(begin, end):
            finish(other, part_at(PLACES[k]), fin_r[k, 0], fin_r[k, 1])
    for present, outward, unused, unused_side in sides:
        @pl.when(present)
        def _(outward=outward):
            outward.wait_send()

    for copy in sends:
        copy.wait_send()


def deliver(new_fields, new_profiles, out_fields, out_profiles, sem):
    copies = []
    for ref, out, rows, pieces in (
        (new_profiles, out_profiles, 512, 6), (new_fields, out_fields, 64, 2),
    ):
        for n in range(pieces):
            part = pl.ds(rows * n, rows)
            copies.append(pltpu.make_async_copy(ref.at[part], out.at[part], sem.at[len(copies)]))
    for copy in copies:
        copy.start()
    for copy in copies:
        copy.wait()


def body(fields, conductance, lateral, partition, arm_step, profiles, tile_ids, tile_count):
    tile = (8, 128)
    scratch = [
        (10, 128, 128), (8, 128, 128), (8, 128, 128), (3072, 128), (32, 9) + tile, (32, 3) + tile,
        (2, 8, 16, 128), (2, 8, 16, 128),
        (16, 3) + tile, (16, 2) + tile, (2, 16, 3) + tile, (2, 16, 2) + tile, (16, 3) + tile,
        (16, 3) + tile, (16, 2) + tile, (16, 3) + tile, (16, 2) + tile,
        (2, 3) + tile, (2, 2) + tile, (2, 3) + tile, (2, 2) + tile,
        (16, 2) + tile, (16, 2) + tile, (2, 16, 2) + tile, (16, 2) + tile, (2, 7, 3) + tile,
        (4, 16, 128), (3, 32, 64), (3, 64, 16), (3, 16, 128), (3, 32, 256), (3, 64, 256),
        (3, 512, 128), (3, 256, 128), (16, 384), (4, 256, 128),
    ]
    hbm = pl.BlockSpec(memory_space=pl.ANY)
    vmem = pl.BlockSpec(memory_space=pltpu.VMEM)
    operands = [
        pltpu.with_memory_space_constraint(x, pltpu.HBM)
        for x in (
            fields.reshape(128, 1024), conductance.reshape(128, 1024), lateral, partition,
            arm_step, profiles.reshape(3072, 128), tile_ids,
        )
    ]
    new_fields, new_profiles = pl.pallas_call(
        functools.partial(kernel, lax.axis_size("xy")),
        out_shape=(pltpu.VMEM((128, 1024), F32), pltpu.VMEM((3072, 128), F32)),
        in_specs=[hbm] * 7 + [pl.BlockSpec(memory_space=pltpu.SMEM)],
        out_specs=(vmem, vmem),
        scratch_shapes=[
            pltpu.SMEM((4,), F32), pltpu.SMEM((3,), F32),
            pltpu.SMEM((1, SLOTS), jnp.int32),
            pltpu.VMEM((1, SLOTS), jnp.int32), pltpu.VMEM((3, ARM, ARM), F32),
        ]
        + [pltpu.VMEM(shape, F32) for shape in scratch]
        + [
            pltpu.SemaphoreType.DMA((16,)),
            pltpu.SemaphoreType.DMA((5,)),
            pltpu.SemaphoreType.DMA((3,)),
            pltpu.SemaphoreType.DMA((56,)),
            pltpu.SemaphoreType.DMA((56,)),
            pltpu.SemaphoreType.REGULAR,
        ],
        compiler_params=pltpu.CompilerParams(
            collective_id=0, has_side_effects=True, vmem_limit_bytes=40 * 2**20
        ),
        cost_estimate=pl.CostEstimate(flops=10**9, bytes_accessed=5 * 2**20, transcendentals=2048),
        name="ingot",
    )(*operands, tile_count)
    new_fields, new_profiles = pl.pallas_call(
        deliver,
        out_shape=(pltpu.HBM((128, 1024), F32), pltpu.HBM((3072, 128), F32)),
        in_specs=[vmem, vmem],
        out_specs=(hbm, hbm),
        scratch_shapes=[pltpu.SemaphoreType.DMA((8,))],
        cost_estimate=pl.CostEstimate(flops=0, bytes_accessed=2**22, transcendentals=0),
        name="deliver",
    )(
        pltpu.with_memory_space_constraint(new_fields, pltpu.VMEM),
        pltpu.with_memory_space_constraint(new_profiles, pltpu.VMEM),
    )
    return new_fields.reshape(fields.shape), new_profiles.reshape(profiles.shape)


def solution(mesh):
    return jax.shard_map(
        body,
        mesh=mesh,
        in_specs=(
            P(None, "gz", "xy", None),
            P(None, "gz", "xy", None),
            P(),
            P(),
            P(),
            P(None, ("gz", "xy"), None, None),
            P(("gz", "xy"), None),
            P(("gz", "xy")),
        ),
        out_specs=(P(None, "gz", "xy", None), P(None, ("gz", "xy"), None, None)),
        check_vma=False,
    )
```

```python
import functools

import jax
import jax.numpy as jnp
from jax import lax
from jax.experimental import pallas as pl
from jax.experimental.pallas import tpu as pltpu
from jax.sharding import PartitionSpec as P

F32 = jnp.float32
BF16 = jnp.bfloat16
MESH = pl.DeviceIdType.MESH
HIGH = lax.Precision.HIGHEST
SUB = 16
ARM = 64
SLOTS = 16
CHIPS = 16
HALF = CHIPS // 2
REACH = 5
KNOWN = 3
TO = [REACH - i for i in range(HALF)] + [2 * REACH - i for i in range(HALF, CHIPS)]
PLACES = sorted(range(CHIPS), key=lambda i: (-abs(TO[i]), i))
SENT = PLACES[:-2]
OUT = ((0, 6), (6, 16))
BACK = ((10, 16), (4, 10), (0, 4))


def merge_mass(low, high):
    mass = low[2] + high[1]
    inverse = 1.0 / (mass + low[0] + high[0])
    a, b = low[0] * inverse, high[0] * inverse
    return (a * high[0], low[1] + a * mass, high[2] + b * mass), (a, b, inverse)


def merge_rhs(low, high, a, b, inverse):
    rhs = low[1] + high[0]
    return (low[0] + a * rhs, high[1] + b * rhs), rhs * inverse


def split(x):
    high = x.astype(BF16).astype(F32)
    return high, x - high


def dot(x, y, precision=None):
    return jnp.dot(x, y, precision=precision, preferred_element_type=F32)


def kernel(
    n_xy,
    fields, cond, lateral_in, partition_in, arm_in, profiles, ids_in, count,
    out_fields, out_profiles,
    lateral, partition, ids, ids_row, arm,
    fld, cnd, src, prof, coef, tail,
    halo_s, halo_r,
    pair_cs, pair_rs, blk_c, blk_r, chip_coef,
    ring_cs, ring_rs, ring_cr, ring_rr, half_cs, half_rs, half_cr, half_rr,
    ret_s, ret_r, fin, fin_r, top_coef,
    cells, wsc, gsc, hsc, lhs1, lhs2, ysc, ssc, change, delta,
    in_sem, small_sem, prof_sem,
    send_sem, recv_sem, near_sem,
):
    gz = lax.axis_index("gz")
    xy = lax.axis_index("xy")
    core = lax.rem(gz, 2)
    chip = gz // 2
    other = 1 - core

    def at_chip(offset):
        return (lax.rem(chip + (offset + CHIPS), CHIPS) * 2 + core, xy)

    left = (gz, lax.rem(xy + n_xy - 1, n_xy))
    right = (gz, lax.rem(xy + 1, n_xy))
    peer = (chip * 2 + other, xy)

    def load(ref, buf, base, y, sem):
        return pltpu.make_async_copy(
            ref.at[:, pl.ds(128 * y, 128)], buf.at[y + base], in_sem.at[sem + y]
        )

    field_loads = [load(fields, fld, 1, y, 0) for y in range(8)]
    cond_loads = [load(cond, cnd, 0, y, 8) for y in range(8)]
    prof_loads = [
        pltpu.make_async_copy(
            profiles.at[pl.ds(1024 * j, 1024)], prof.at[pl.ds(1024 * j, 1024)], prof_sem.at[j]
        )
        for j in range(3)
    ]
    small = [(lateral_in, lateral), (partition_in, partition), (ids_in, ids)]
    small += [(ids_in, ids_row), (arm_in, arm)]
    small_loads = [
        pltpu.make_async_copy(ref, buf, small_sem.at[n]) for n, (ref, buf) in enumerate(small)
    ]
    barrier = pltpu.get_barrier_semaphore()
    has_left, has_right = xy > 0, xy < n_xy - 1

    partners = [at_chip(d * sign) for d in range(KNOWN, 0, -1) for sign in (1, -1)] + [peer]
    for partner in partners:
        pl.semaphore_signal(barrier, inc=1, device_id=partner, device_id_type=MESH)
    @pl.when(has_left)
    def _():
        pl.semaphore_signal(barrier, inc=1, device_id=left, device_id_type=MESH)

    @pl.when(has_right)
    def _():
        pl.semaphore_signal(barrier, inc=1, device_id=right, device_id_type=MESH)

    for copy in field_loads + cond_loads + small_loads:
        copy.start()

    sends = []
    used = [0]

    def describe(source, target, device):
        n = used[0]
        used[0] = n + 1
        return pltpu.make_async_remote_copy(
            src_ref=source, dst_ref=target, send_sem=send_sem.at[n], recv_sem=recv_sem.at[n],
            device_id=device, device_id_type=MESH,
        )

    def remote(source, target, device):
        copy = describe(source, target, device)
        copy.start()
        sends.append(copy)
        return copy

    fld[0] = jnp.zeros((128, 128), F32)
    fld[9] = jnp.zeros((128, 128), F32)
    for copy in field_loads:
        copy.wait()
    for y in range(8):
        halo_s[0, y] = fld[y + 1, pl.ds(0, 16, stride=8), :]
        halo_s[1, y] = fld[y + 1, pl.ds(7, 16, stride=8), :]
    keep = jnp.where(gz == lax.axis_size("gz") - 1, 0.0, 1.0).astype(F32)
    for copy in cond_loads:
        copy.wait()

    def plane(buf, y, f, z):
        return buf[y, pl.ds(pl.multiple_of(f * 32 + z * 8, 8), 8), :]

    def eliminate_mass(owner, p):
        f, y = owner * 2 + p // 8, lax.rem(p, 8)
        e = owner * 16 + p
        block = (plane(cnd, y, f, 0), 1.0, 0.0)
        for z in (1, 2, 3):
            face = plane(cnd, y, f, z)
            if z == 3:
                face = face * keep
            block, held = merge_mass(block, (face, 1.0, 0.0))
            for n in range(3):
                coef[e, 3 * z - 3 + n] = held[n]
        return block

    @pl.loop(0, 16, unroll=4)
    def _(p):
        block = eliminate_mass(other, p)
        for n in range(3):
            pair_cs[p, n] = block[n]

    edges = lax.min(xy, 1) + lax.min(n_xy - 1 - xy, 1)
    pl.semaphore_wait(barrier, len(partners) + edges)
    for sign in (1, -1):
        pl.semaphore_signal(
            near_sem, inc=1, device_id=at_chip(sign * (REACH - KNOWN)), device_id_type=MESH
        )
    to_left = describe(halo_s.at[0], halo_r.at[1], left)
    to_right = describe(halo_s.at[1], halo_r.at[0], right)
    sides = ((has_left, to_left, to_right, 0), (has_right, to_right, to_left, 1))
    for present, outward, unused, unused_side in sides:
        @pl.when(present)
        def _(outward=outward):
            outward.start()

    pair_c = remote(pair_cs, blk_c.at[core], peer)

    @pl.loop(0, 16, unroll=4)
    def _(p):
        block = eliminate_mass(core, p)
        for n in range(3):
            blk_c[core, p, n] = block[n]

    def powers(j):
        power = arm[j]
        wsc[j] = jnp.full((32, ARM), 1.0 / ARM, F32)
        last = lax.broadcasted_iota(jnp.int32, (ARM, SUB), 0) == ARM - 1
        gsc[j] = jnp.where(last, 1.0, 0.0).astype(F32)
        n = 1
        while n < SUB:
            both = dot(jnp.concatenate([power, wsc[j, 0:8]], axis=0), power, HIGH)
            tips = dot(power, gsc[j], HIGH)
            wsc[j, n : 2 * n] = both[ARM : ARM + n]
            gsc[j, :, n : 2 * n] = tips[:, 0:n]
            power = both[:ARM]
            n *= 2
        wsc[j, SUB : SUB + 1] = jnp.sum(power, axis=0, keepdims=True) * (1.0 / ARM)
        rows = wsc[j]
        end = lax.broadcasted_iota(jnp.int32, (SUB, ARM), 1) == ARM - 1
        held = jnp.sum(jnp.where(end, rows[:SUB], 0.0), axis=1, keepdims=True)
        hsc[j] = jnp.broadcast_to(held, (SUB, 128))
        for n, part in enumerate(split(rows)):
            lhs1[j, :, 128 * n : 128 * n + 64] = part
            lhs1[j, :, 128 * n + 64 : 128 * n + 128] = part
        high, low = split(power)
        lhs2[j, :, 0:64] = high
        lhs2[j, :, 64:128] = high
        lhs2[j, :, 128:192] = low
        high, low = split(gsc[j])
        lhs2[j, :, 192:208] = high
        lhs2[j, :, 208:224] = high
        lhs2[j, :, 224:240] = low
        lhs2[j, :, 240:256] = low

    def part_at(i):
        return lax.rem(chip + (CHIPS - i), CHIPS)

    pair_c.wait_recv()
    for i in range(CHIPS):
        p = part_at(i)
        merged, held = merge_mass(*([blk_c[c, p, n] for n in range(3)] for c in range(2)))
        target = ring_cs if TO[i] else ring_cr
        for n in range(3):
            chip_coef[i, n] = held[n]
            target[i, n] = merged[n]
    def send_mass(far):
        return [
            remote(ring_cs.at[i], ring_cr.at[i], at_chip(TO[i]))
            for i in SENT
            if (abs(TO[i]) > KNOWN) == far
        ]

    ring_c = send_mass(False)
    pl.semaphore_wait(near_sem, 2)
    ring_c += send_mass(True)


    for copy in prof_loads:
        copy.start()

    for copy in small_loads:
        copy.wait()
    row = lax.broadcasted_iota(jnp.int32, (8, 128), 0)
    lane = lax.broadcasted_iota(jnp.int32, (8, 128), 1)

    @pl.loop(0, 16)
    def _(q):
        at = pl.ds(pl.multiple_of(q * 8, 8), 8)
        rate = lateral[q // 4]
        tiles = [fld[y, at, :] for y in range(10)]
        for y in range(8):
            before, here, after = tiles[y : y + 3]
            down = jnp.where(row == 0, 0.0, pltpu.roll(here, 1, 0))
            up = jnp.where(row == 7, 0.0, pltpu.roll(here, 7, 0))
            low = pltpu.roll(jnp.where(lane == 127, before, here), 1, 1)
            high = pltpu.roll(jnp.where(lane == 0, after, here), 127, 1)
            src[y, at, :] = here + rate * (down + up + low + high - 4.0 * here)

    for present, unused, inward, side in sides:
        @pl.when(present)
        def _(inward=inward):
            inward.wait_recv()

        @pl.when(jnp.logical_not(present))
        def _(side=side):
            halo_r[side] = jnp.zeros((8, 16, 128), F32)

    def eliminate_rhs(owner, p):
        f, y = owner * 2 + p // 8, lax.rem(p, 8)
        e = owner * 16 + p
        rate = lateral[f]
        block = None
        for z in range(4):
            edge = jnp.where(row == 0, halo_r[0, y, pl.ds(f * 4 + z, 1), :] * rate, 0.0)
            edge += jnp.where(row == 7, halo_r[1, y, pl.ds(f * 4 + z, 1), :] * rate, 0.0)
            here = plane(src, y, f, z) + edge
            if z == 0:
                block = (here, 0.0)
            else:
                block, tail[e, z - 1] = merge_rhs(
                    block, (here, 0.0), *(coef[e, 3 * z - 3 + n] for n in range(3))
                )
        return block

    pair_r = []
    for begin, end in OUT:
        for k in range(begin, end):
            block = eliminate_rhs(other, part_at(PLACES[k]))
            for n in range(2):
                pair_rs[k, n] = block[n]
        piece = pl.ds(begin, end - begin)
        pair_r.append(remote(pair_rs.at[piece], blk_r.at[core, piece], peer))
    for k in range(CHIPS):
        block = eliminate_rhs(core, part_at(PLACES[k]))
        for n in range(2):
            blk_r[core, k, n] = block[n]

    ring_r = []
    for copy, (begin, end) in zip(pair_r, OUT):
        copy.wait_recv()
        for k in range(begin, end):
            i = PLACES[k]
            merged, chip_coef[i, 2] = merge_rhs(
                *([blk_r[c, k, n] for n in range(2)] for c in range(2)),
                *(chip_coef[i, n] for n in range(3)),
            )
            target = ring_rs if TO[i] else ring_rr
            for n in range(2):
                target[i, n] = merged[n]
        for i in PLACES[begin:end]:
            if TO[i]:
                ring_r.append(remote(ring_rs.at[i], ring_rr.at[i], at_chip(TO[i])))

    for j in range(3):
        powers(j)


    for copy in ring_c:
        copy.wait_recv()
    for half in range(2):
        masses = [[ring_cr[half * HALF + b, n] for n in range(3)] for b in range(HALF)]
        at = 0
        while len(masses) > 1:
            joined = [merge_mass(*masses[b : b + 2]) for b in range(0, len(masses), 2)]
            masses = [block for block, held in joined]
            for block, held in joined:
                for n in range(3):
                    top_coef[half, at, n] = held[n]
                at += 1
        for n in range(3):
            half_cs[half, n] = masses[0][n]
    across = (at_chip(REACH), at_chip(-REACH))
    half_c = [remote(half_cs.at[h], half_cr.at[1 - h], across[h]) for h in range(2)]

    for copy in prof_loads:
        copy.wait()

    def tile_pair(j, t):
        at = [pl.multiple_of(j * 1024 + t * 128 + 64 * n, 64) for n in range(2)]
        return at, jnp.concatenate([prof[pl.ds(a, 64), :] for a in at], axis=1)

    @pl.loop(0, 8)
    def _(t):
        for j in range(3):
            unused, tile = tile_pair(j, t)
            high, low = (part.astype(BF16) for part in split(tile))
            means = dot(lhs1[j].astype(BF16), jnp.concatenate([high, low, high, low], axis=0))
            for n in range(2):
                ysc[j, pl.ds(pl.multiple_of(t * 64 + 32 * n, 32), 32), :] = means[:, 128 * n : 128 * n + 128]

    for slot in range(SLOTS):
        tile = ids[0, slot]
        y, at = lax.rem(tile, 8), (tile // 64) * 8 + lax.rem(tile // 8, 8)
        for f in range(4):
            cells[f, slot : slot + 1] = fld[y + 1, pl.ds(f * 32 + at, 1), :]

    live = lax.broadcasted_iota(jnp.int32, (SLOTS, 128), 0) < count[0]
    solid = 0.9 / (1.0 + jnp.exp(cells[3]))
    inverses = [1.0 / (1.0 - solid * ((k + 1) / SUB)) for k in range(SUB)]
    for j in range(3):
        solute = cells[j]
        half = 0.5 * partition[j]
        liquids = []
        for k in range(SUB + 1):
            mean = ysc[j, pl.ds(k, SLOTS, stride=32), :]
            for i in range(k):
                mean += hsc[j, k - 1 - i : k - i, :] * liquids[i]
            if k == SUB:
                moved = solid * (mean - partition[j] * solute)
                change[:, 128 * j : 128 * j + 128] = jnp.where(live, moved, 0.0)
            else:
                fraction = solid * ((k + 1) / SUB)
                liquids.append(half * ((solute - fraction * mean) * inverses[k]))
                ssc[j, pl.ds(SUB - 1 - k, SLOTS, stride=SUB), :] = liquids[k]

    for copy in ring_r:
        copy.wait_recv()
    levels = ([], [])
    for half in range(2):
        rhs = [[ring_rr[half * HALF + b, n] for n in range(2)] for b in range(HALF)]
        at = 0
        while len(rhs) > 1:
            level, joined = [], []
            for b in range(0, len(rhs), 2):
                block, top_coef[half, at, 2] = merge_rhs(
                    rhs[b], rhs[b + 1], *(top_coef[half, at, n] for n in range(3))
                )
                joined.append(block)
                level.append(at)
                at += 1
            rhs = joined
            levels[half].append(level)
        for n in range(2):
            half_rs[half, n] = rhs[0][n]
    half_r = [remote(half_rs.at[h], half_rr.at[1 - h], across[h]) for h in range(2)]

    def evolve(j):
        @pl.loop(0, 8)
        def _(t):
            at, tile = tile_pair(j, t)
            tips = jnp.concatenate(
                [ssc[j, pl.ds(pl.multiple_of(t * 32 + 16 * n, 16), 16), :] for n in range(2)], axis=1
            )
            high, low = (part.astype(BF16) for part in split(tile))
            tip_high, tip_low = (part.astype(BF16) for part in split(tips))
            evolved = dot(
                lhs2[j].astype(BF16),
                jnp.concatenate(
                    [high, low, high, tip_high, tip_low, tip_high, tip_low], axis=0
                ),
            )
            for n in range(2):
                shown = jnp.full((ARM, 128), 2 * t + n, jnp.int32) < count[0]
                out_profiles[pl.ds(at[n], 64), :] = jnp.where(
                    shown, evolved[:, 128 * n : 128 * n + 128], 0.0
                )

    evolve(0)

    for copy in half_c + half_r:
        copy.wait_recv()
    for half in range(2):
        own, met = (half_cs, half_rs), (half_cr, half_rr)
        lower, upper = (own, met) if half == 0 else (met, own)
        whole, held = merge_mass(*([buf[0][half, n] for n in range(3)] for buf in (lower, upper)))
        total, ratio = merge_rhs(
            *([buf[1][half, n] for n in range(2)] for buf in (lower, upper)), *held
        )
        start = (total[0] + total[1]) / (whole[1] + whole[2])
        middle = ratio + (held[0] + held[1]) * start
        values = [start, middle] if half == 0 else [middle, start]
        for level in reversed(levels[half]):
            finer = [values[0]]
            for b, at in enumerate(level):
                a, c, ratio = (top_coef[half, at, n] for n in range(3))
                finer += [ratio + a * values[b] + c * values[b + 1], values[b + 1]]
            values = finer
        for b in range(HALF):
            i = half * HALF + b
            target = ret_s if TO[i] else ret_r
            for n in range(2):
                target[i, n] = values[b + n]
    ret = {i: remote(ret_s.at[i], ret_r.at[i], at_chip(-TO[i])) for i in SENT}

    evolve(1)
    evolve(2)

    place = lax.broadcasted_iota(jnp.int32, (256, SLOTS), 0)
    named = (place // 64) * 64 + lax.rem(place, 8) * 8 + lax.rem(place // 8, 8)
    hit = jnp.where(named == ids_row[...], 1.0, 0.0).astype(BF16)
    rest = change[...]
    spreads = None
    for n in range(3):
        piece = rest.astype(BF16)
        rest = rest - piece.astype(F32)
        term = dot(hit, piece)
        spreads = term if spreads is None else spreads + term
    for j in range(3):
        delta[j] = spreads[:, 128 * j : 128 * j + 128]
    delta[3] = jnp.zeros((256, 128), F32)

    def finish(owner, p, low, high):
        f, y = owner * 2 + p // 8, lax.rem(p, 8)
        e = owner * 16 + p
        above = high
        values = [low, None, None, None]
        for z in (3, 2, 1):
            above = tail[e, z - 1] + coef[e, 3 * z - 3] * low + coef[e, 3 * z - 2] * above
            values[z] = above
        lanes = pl.ds(pl.multiple_of(y * 128, 128), 128)
        for z in range(4):
            at = pl.ds(pl.multiple_of(f * 32 + z * 8, 8), 8)
            out_fields[at, lanes] = values[z] + delta[f, pl.ds(pl.multiple_of(z * 64 + y * 8, 8), 8), :]

    last = []
    for begin, end in BACK:
        for i in PLACES[begin:end]:
            if TO[i]:
                ret[i].wait_recv()
        for k in range(begin, end):
            i = PLACES[k]
            low, high = ret_r[i, 0], ret_r[i, 1]
            middle = chip_coef[i, 2] + chip_coef[i, 0] * low + chip_coef[i, 1] * high
            fin[0, k, 0] = low
            fin[0, k, 1] = middle
            fin[1, k, 0] = middle
            fin[1, k, 1] = high
        piece = pl.ds(begin, end - begin)
        last.append(remote(fin.at[other, piece], fin_r.at[piece], peer))
        for k in range(begin, end):
            finish(core, part_at(PLACES[k]), fin[core, k, 0], fin[core, k, 1])
    for copy, (begin, end) in zip(last, BACK):
        copy.wait_recv()
        for k in range(begin, end):
            finish(other, part_at(PLACES[k]), fin_r[k, 0], fin_r[k, 1])
    for present, outward, unused, unused_side in sides:
        @pl.when(present)
        def _(outward=outward):
            outward.wait_send()

    for copy in sends:
        copy.wait_send()


def deliver(new_fields, new_profiles, out_fields, out_profiles, sem):
    copies = []
    for ref, out, rows, pieces in (
        (new_profiles, out_profiles, 512, 6), (new_fields, out_fields, 64, 2),
    ):
        for n in range(pieces):
            part = pl.ds(rows * n, rows)
            copies.append(pltpu.make_async_copy(ref.at[part], out.at[part], sem.at[len(copies)]))
    for copy in copies:
        copy.start()
    for copy in copies:
        copy.wait()


def body(fields, conductance, lateral, partition, arm_step, profiles, tile_ids, tile_count):
    tile = (8, 128)
    scratch = [
        (10, 128, 128), (8, 128, 128), (8, 128, 128), (3072, 128), (32, 9) + tile, (32, 3) + tile,
        (2, 8, 16, 128), (2, 8, 16, 128),
        (16, 3) + tile, (16, 2) + tile, (2, 16, 3) + tile, (2, 16, 2) + tile, (16, 3) + tile,
        (16, 3) + tile, (16, 2) + tile, (16, 3) + tile, (16, 2) + tile,
        (2, 3) + tile, (2, 2) + tile, (2, 3) + tile, (2, 2) + tile,
        (16, 2) + tile, (16, 2) + tile, (2, 16, 2) + tile, (16, 2) + tile, (2, 7, 3) + tile,
        (4, 16, 128), (3, 32, 64), (3, 64, 16), (3, 16, 128), (3, 32, 256), (3, 64, 256),
        (3, 512, 128), (3, 256, 128), (16, 384), (4, 256, 128),
    ]
    hbm = pl.BlockSpec(memory_space=pl.ANY)
    vmem = pl.BlockSpec(memory_space=pltpu.VMEM)
    operands = [
        pltpu.with_memory_space_constraint(x, pltpu.HBM)
        for x in (
            fields.reshape(128, 1024), conductance.reshape(128, 1024), lateral, partition,
            arm_step, profiles.reshape(3072, 128), tile_ids,
        )
    ]
    new_fields, new_profiles = pl.pallas_call(
        functools.partial(kernel, lax.axis_size("xy")),
        out_shape=(pltpu.VMEM((128, 1024), F32), pltpu.VMEM((3072, 128), F32)),
        in_specs=[hbm] * 7 + [pl.BlockSpec(memory_space=pltpu.SMEM)],
        out_specs=(vmem, vmem),
        scratch_shapes=[
            pltpu.SMEM((4,), F32), pltpu.SMEM((3,), F32),
            pltpu.SMEM((1, SLOTS), jnp.int32),
            pltpu.VMEM((1, SLOTS), jnp.int32), pltpu.VMEM((3, ARM, ARM), F32),
        ]
        + [pltpu.VMEM(shape, F32) for shape in scratch]
        + [
            pltpu.SemaphoreType.DMA((16,)),
            pltpu.SemaphoreType.DMA((5,)),
            pltpu.SemaphoreType.DMA((3,)),
            pltpu.SemaphoreType.DMA((56,)),
            pltpu.SemaphoreType.DMA((56,)),
            pltpu.SemaphoreType.REGULAR,
        ],
        compiler_params=pltpu.CompilerParams(
            collective_id=0, has_side_effects=True, vmem_limit_bytes=40 * 2**20
        ),
        cost_estimate=pl.CostEstimate(flops=10**9, bytes_accessed=5 * 2**20, transcendentals=2048),
        name="ingot",
    )(*operands, tile_count)
    new_fields, new_profiles = pl.pallas_call(
        deliver,
        out_shape=(pltpu.HBM((128, 1024), F32), pltpu.HBM((3072, 128), F32)),
        in_specs=[vmem, vmem],
        out_specs=(hbm, hbm),
        scratch_shapes=[pltpu.SemaphoreType.DMA((8,))],
        cost_estimate=pl.CostEstimate(flops=0, bytes_accessed=2**22, transcendentals=0),
        name="deliver",
    )(
        pltpu.with_memory_space_constraint(new_fields, pltpu.VMEM),
        pltpu.with_memory_space_constraint(new_profiles, pltpu.VMEM),
    )
    return new_fields.reshape(fields.shape), new_profiles.reshape(profiles.shape)


def solution(mesh):
    return jax.shard_map(
        body,
        mesh=mesh,
        in_specs=(
            P(None, "gz", "xy", None),
            P(None, "gz", "xy", None),
            P(),
            P(),
            P(),
            P(None, ("gz", "xy"), None, None),
            P(("gz", "xy"), None),
            P(("gz", "xy")),
        ),
        out_specs=(P(None, "gz", "xy", None), P(None, ("gz", "xy"), None, None)),
        check_vma=False,
    )
```
